32 devices in a mesh: seq: 4 (over x, core), ctx: 8 (over z, y).
Axes of the slice: x: 2, y: 2, z: 4, core: 2. Of those that a mesh axis runs over, the one named last changes fastest.
Arguments:
- tokens: bfloat16 [4096, 1536], P(('seq', 'ctx')), may hold values from -6 to 6
- segments: int32 [4, 1024], P('seq'), may hold values from 0 to 1023, as said below
- w_query: bfloat16 [1536, 1536], P(('seq', 'ctx')), may hold values from -0.15625 to 0.15625
- b_query: bfloat16 [1536], P(('seq', 'ctx')), may hold values from -3 to 3
- w_key: bfloat16 [1536, 256], P(('seq', 'ctx')), may hold values from -0.15625 to 0.15625
- b_key: bfloat16 [256], replicated, may hold values from -3 to 3
- w_value: bfloat16 [1536, 256], P(('seq', 'ctx')), may hold values from -0.15625 to 0.15625
- b_value: bfloat16 [256], P(('seq', 'ctx')), may hold values from -3 to 3
- w_out: bfloat16 [1536, 1536], P(('seq', 'ctx')), may hold values from -0.3125 to 0.3125
- norm_attn: bfloat16 [1536], P(('seq', 'ctx')), may hold values from 0.25 to 1.75
- w_gate: bfloat16 [1536, 8960], P(('seq', 'ctx')), may hold values from -0.15625 to 0.15625
- w_up: bfloat16 [1536, 8960], P(('seq', 'ctx')), may hold values from -0.15625 to 0.15625
- w_down: bfloat16 [8960, 1536], P(('seq', 'ctx')), may hold values from -0.0625 to 0.0625
- norm_mlp: bfloat16 [1536], P(('seq', 'ctx')), may hold values from 0.25 to 1.75
- cotangent: bfloat16 [4096, 1536], P(('seq', 'ctx')), may hold values from -6 to 6
Outputs:
- output: float32 [4096, 1536], P(('seq', 'ctx'))
- grad_tokens: float32 [4096, 1536], P(('seq', 'ctx'))
- grad_w_query: float32 [1536, 1536], P(('seq', 'ctx'))
- grad_b_query: float32 [1536], P(('seq', 'ctx'))
- grad_w_key: float32 [1536, 256], P(('seq', 'ctx'))
- grad_b_key: float32 [256], replicated
- grad_w_value: float32 [1536, 256], P(('seq', 'ctx'))
- grad_b_value: float32 [256], P(('seq', 'ctx'))
- grad_w_out: float32 [1536, 1536], P(('seq', 'ctx'))
- grad_norm_attn: float32 [1536], P(('seq', 'ctx'))
- grad_w_gate: float32 [1536, 8960], P(('seq', 'ctx'))
- grad_w_up: float32 [1536, 8960], P(('seq', 'ctx'))
- grad_w_down: float32 [8960, 1536], P(('seq', 'ctx'))
- grad_norm_mlp: float32 [1536], P(('seq', 'ctx'))
The draws below stay inside these ranges and needn't reach their ends.
Inputs may be any that keep to these rules, and one draw needn't show every extreme that they name: `segments`: within each sequence the ids never fall, and a document's id is the place of its first token. One sequence, which one drawn from the seed, is a single document of 1024 tokens; in every other sequence the last token is a document of its own.
All inputs are finite; a program needn't handle non-finite values.
Results may differ from the reference program's by a relative error of at most 0.033.
Values may be sent and summed in bfloat16 or wider, within the bound.
No kernel may reach another device: no remote copies, remote signals or barrier semaphores. Data moves between devices by JAX's collectives and lax.ppermute only.
A program may use at most 512 MiB of HBM per device.

```python
import math
from functools import partial
import jax
import jax.numpy as jnp
from jax import lax

HEADS = 12
KV_HEADS = 2
HEAD_DIM = 128
FFN = 8960
WIDTH = 1536
KV_WIDTH = 256
SEQ_LEN = 1024
SEQS = 4
TOKENS = 4096


def draw_segments(key, part):
    rate_key = jax.random.fold_in(key, 11)
    coin_key = jax.random.fold_in(key, 12)
    pick_key = jax.random.fold_in(key, 13)
    rates = jax.random.randint(rate_key, (SEQS, 1), 1, 9)
    coins = jax.random.randint(coin_key, (SEQS, SEQ_LEN), 0, 256)
    index = jnp.arange(SEQ_LEN, dtype=jnp.int32)
    flags = (coins < rates) | (index[None, :] == 0) | (index[None, :] == SEQ_LEN - 1)
    firsts = lax.cummax(jnp.where(flags, index[None, :], 0).astype(jnp.int32), axis=1)
    whole = jax.random.randint(pick_key, (), 0, SEQS)
    rows = jnp.arange(SEQS, dtype=jnp.int32)[:, None]
    return jnp.where(rows == whole, 0, firsts).astype(jnp.int32)


def levels(own_key, dims, split, smallest, high):
    def one(dim, parts):
        draws = jax.random.uniform(jax.random.fold_in(jax.random.fold_in(own_key, 6), dim), (parts,), jnp.float32, smallest / len(split), high / len(split))
        return jnp.repeat(jnp.exp(draws), dims[dim] // parts).reshape((-1,) + (1,) * (len(dims) - dim - 1))

    factor_of = one(*split[0])
    for cut in split[1:]:
        factor_of = factor_of * one(*cut)
    return factor_of


def scatter_about(own_key, dims, deviation, reach, pieces=(), kind=jnp.bfloat16):
    factor_of = levels(own_key, dims, pieces, -0.22, 0.18) if pieces else 1.0
    array = jax.random.normal(own_key, dims, jnp.float32) * deviation * factor_of
    return jnp.minimum(jnp.maximum(array, -reach), reach).astype(kind)


def setup_inputs(seed: int = 0) -> dict:
    streams_of = jax.random.split(jax.random.key(seed), 16)
    return {
        "tokens": scatter_about(streams_of[0], (TOKENS, WIDTH), 1.0, 6.0, ((0, 32),)),
        "segments": draw_segments(jax.random.fold_in(streams_of[15], 71), 0),
        "w_query": scatter_about(streams_of[2], (WIDTH, WIDTH), WIDTH ** -0.5, 0.15625, ((0, 32),)),
        "b_query": scatter_about(streams_of[3], (WIDTH,), 0.5, 3.0, ((0, 32),)),
        "w_key": scatter_about(streams_of[4], (WIDTH, KV_WIDTH), WIDTH ** -0.5, 0.15625, ((0, 32),)),
        "b_key": scatter_about(streams_of[5], (KV_WIDTH,), 0.5, 3.0),
        "w_value": scatter_about(streams_of[6], (WIDTH, KV_WIDTH), WIDTH ** -0.5, 0.15625, ((0, 32),)),
        "b_value": scatter_about(streams_of[7], (KV_WIDTH,), 0.5, 3.0, ((0, 32),)),
        "w_out": scatter_about(streams_of[8], (WIDTH, WIDTH), (WIDTH // 4) ** -0.5, 0.3125, ((0, 32),)),
        "norm_attn": jnp.clip(1.0 + 0.15 * jax.random.normal(streams_of[9], (WIDTH,), jnp.float32), 0.25, 1.75).astype(jnp.bfloat16),
        "w_gate": scatter_about(streams_of[10], (WIDTH, FFN), WIDTH ** -0.5, 0.15625, ((0, 32),)),
        "w_up": scatter_about(streams_of[11], (WIDTH, FFN), WIDTH ** -0.5, 0.15625, ((0, 32),)),
        "w_down": scatter_about(streams_of[12], (FFN, WIDTH), FFN ** -0.5, 0.0625, ((0, 32),)),
        "norm_mlp": jnp.clip(1.0 + 0.15 * jax.random.normal(streams_of[13], (WIDTH,), jnp.float32), 0.25, 1.75).astype(jnp.bfloat16),
        "cotangent": scatter_about(streams_of[14], (TOKENS, WIDTH), 1.0, 6.0, ((0, 32),)),
    }


EPS = 1e-06
THETA = 1000000.0

@jax.custom_vjp
def low(v):
    return lax.optimization_barrier(v.astype(jnp.bfloat16)).astype(jnp.float32)

@jax.custom_vjp
def low_back(v):
    return v

def low_keep(v):
    return (low(v), None)

def low_pass(kept, grad):
    return (grad,)

def back_keep(v):
    return (v, None)

def back_low(kept, grad):
    return (low(grad),)
low.defvjp(low_keep, low_pass)
low_back.defvjp(back_keep, back_low)

def doc_positions(ident):
    length = ident.shape[0]
    index = jnp.arange(length, dtype=jnp.int32)
    boundary = jnp.concatenate([jnp.ones((1,), jnp.bool_), ident[1:] != ident[:-1]])
    first = lax.cummax(jnp.where(boundary, index, 0).astype(jnp.int32), axis=0)
    return index - first

def rope_tables(positions):
    half = HEAD_DIM // 2
    freqs = THETA ** (-(2.0 * jnp.arange(half, dtype=jnp.float32)) / HEAD_DIM)
    angles = positions.astype(jnp.float32)[:, None] * freqs[None, :]
    cosine = jnp.concatenate([jnp.cos(angles), jnp.cos(angles)], axis=-1)[:, None, :]
    sine = jnp.concatenate([jnp.sin(angles), jnp.sin(angles)], axis=-1)[:, None, :]
    return (cosine, sine)

def rotate(values, cosine, sine, sign):
    half = values.shape[-1] // 2
    turned = jnp.concatenate([-values[..., half:], values[..., :half]], axis=-1)
    return values * cosine + sign * turned * sine

def inverse_rms(values):
    return lax.rsqrt(lax.optimization_barrier(jnp.mean(values * values, axis=-1, keepdims=True)) + EPS)

def dot_high(left, right):
    return jnp.dot(left, right, precision=lax.Precision.HIGHEST, preferred_element_type=jnp.float32)

def attend_block(query_block, start, keys, values, ident):
    rows = query_block.shape[0]
    group = HEADS // KV_HEADS
    query_group = query_block.reshape(rows, KV_HEADS, group, HEAD_DIM)
    scores = jnp.einsum('qkgd,skd->kgqs', query_group, keys, precision=lax.Precision.HIGHEST) * HEAD_DIM ** (-0.5)
    scores = low_back(scores)
    query_index = start + jnp.arange(rows, dtype=jnp.int32)
    key_index = jnp.arange(keys.shape[0], dtype=jnp.int32)
    query_ids = lax.dynamic_slice_in_dim(ident, start, rows)
    allowed = (key_index[None, :] <= query_index[:, None]) & (ident[None, :] == query_ids[:, None])
    shares = jax.nn.softmax(jnp.where(allowed, scores, -1e+30), axis=-1)
    mixed = jnp.einsum('kgqs,skd->qkgd', low(shares), values, precision=lax.Precision.HIGHEST)
    return mixed.reshape(rows, HEADS * HEAD_DIM)

def attend_sequence(items):
    queries, keys, values, ident = items
    block = math.gcd(512, SEQ_LEN)
    count = SEQ_LEN // block
    starts = jnp.arange(count, dtype=jnp.int32) * block
    blocks = queries.reshape(count, block, HEADS, HEAD_DIM)
    stepper = jax.checkpoint(partial(attend_block, keys=keys, values=values, ident=ident))
    result = lax.map(lambda pair: stepper(pair[0], pair[1]), (blocks, starts))
    return result.reshape(SEQ_LEN, WIDTH)

def layer(inputs, params, segments, cosine, sine):
    query_weight, query_bias, key_weight, key_bias, value_weight, value_bias, out_weight, attn_gain, gate_weight, up_weight, down_weight, mlp_gain = params
    normed = low(inputs * inverse_rms(inputs) * attn_gain)
    query_pre = low_back(dot_high(normed, query_weight) + query_bias)
    key_pre = low_back(dot_high(normed, key_weight) + key_bias)
    value = low(low_back(dot_high(normed, value_weight) + value_bias))
    queries = low(rotate(query_pre.reshape(TOKENS, HEADS, HEAD_DIM), cosine, sine, 1.0))
    keys = low(rotate(key_pre.reshape(TOKENS, KV_HEADS, HEAD_DIM), cosine, sine, 1.0))
    values = value.reshape(TOKENS, KV_HEADS, HEAD_DIM)
    mixed = lax.map(attend_sequence, (queries.reshape(SEQS, SEQ_LEN, HEADS, HEAD_DIM), keys.reshape(SEQS, SEQ_LEN, KV_HEADS, HEAD_DIM), values.reshape(SEQS, SEQ_LEN, KV_HEADS, HEAD_DIM), segments))
    mixed = low(low_back(mixed.reshape(TOKENS, WIDTH)))
    middle = inputs + low_back(dot_high(mixed, out_weight))
    normed_mlp = low(middle * inverse_rms(middle) * mlp_gain)
    gate = low_back(dot_high(normed_mlp, gate_weight))
    upper = low_back(dot_high(normed_mlp, up_weight))
    hidden = low(jax.nn.silu(gate) * upper)
    return middle + low_back(dot_high(hidden, down_weight))

def reference(tokens, segments, w_query, b_query, w_key, b_key, w_value, b_value, w_out, norm_attn, w_gate, w_up, w_down, norm_mlp, cotangent):
    positions = jax.vmap(doc_positions)(segments).reshape(TOKENS)
    cosine, sine = rope_tables(positions)
    params = tuple((member.astype(jnp.float32) for member in (w_query, b_query, w_key, b_key, w_value, b_value, w_out, norm_attn, w_gate, w_up, w_down, norm_mlp)))
    inputs = tokens.astype(jnp.float32)

    def forward(values, weights):
        return layer(values, weights, segments, cosine, sine)
    result, pullback = jax.vjp(forward, inputs, params)
    grad_inputs, grads = pullback(cotangent.astype(jnp.float32))
    return (result, grad_inputs, grads[0], grads[1], grads[2], grads[3], grads[4], grads[5], grads[6], grads[7], grads[8], grads[9], grads[10], grads[11])
```

```python
import functools

import jax
import jax.numpy as jnp
from jax import lax
from jax.experimental import pallas as pl
from jax.experimental.pallas import tpu as pltpu
from jax.sharding import PartitionSpec as P

HEADS = 12
KV_HEADS = 2
HEAD_DIM = 128
WIDTH = 1536
KV_WIDTH = 256
GROUP = HEADS // KV_HEADS
QKV = WIDTH + 2 * KV_WIDTH

EPS = 1e-06
THETA = 1000000.0
NEGATIVE = -1e30
FACTOR = HEAD_DIM ** (-0.5)
VMEM_LIMIT = 56 * 1024 * 1024

ALL = ("seq", "ctx")
BF = jnp.bfloat16
F32 = jnp.float32


def rope_tables(positions):
    half = HEAD_DIM // 2
    freqs = THETA ** (-(2.0 * jnp.arange(half, dtype=F32)) / HEAD_DIM)
    angles = positions.astype(F32)[:, None] * freqs[None, :]
    cosine, sine = jnp.cos(angles), jnp.sin(angles)
    cosine = jnp.concatenate([cosine, cosine], axis=-1)
    sine = jnp.concatenate([sine, sine], axis=-1)
    return cosine, sine


def rotate(values, cosine, sine, sign):
    rows, width = values.shape
    split = values.reshape(rows, width // HEAD_DIM, HEAD_DIM)
    half = HEAD_DIM // 2
    turned = jnp.concatenate([-split[..., half:], split[..., :half]], axis=-1)
    out = split * cosine[:, None, :] + sign * turned * sine[:, None, :]
    return out.reshape(rows, width)


def inverse_rms(values):
    return lax.rsqrt(jnp.mean(values * values, axis=-1, keepdims=True) + EPS)


def matmul(left, right):
    return jnp.dot(left, right, preferred_element_type=F32)


def against(left, weight):
    return lax.dot_general(left, weight, (((1,), (1,)), ((), ())), preferred_element_type=F32)


def outer(left, right):
    return lax.dot_general(left, right, (((0,), (0,)), ((), ())), preferred_element_type=F32)


def allowed_of(lo_ref, hi_ref, rows, length):
    places = lax.broadcasted_iota(jnp.int32, (rows, length), 1)
    return (places >= lo_ref[...]) & (places <= hi_ref[...])


def forward_kernel(q_ref, k_ref, v_ref, lo_ref, hi_ref, mixed_ref, logsum_ref):
    scores = against(q_ref[...], k_ref[...]) * FACTOR
    allowed = allowed_of(lo_ref, hi_ref, *scores.shape)
    scores = jnp.where(allowed, scores, NEGATIVE)
    top = jnp.max(scores, axis=-1, keepdims=True)
    weights = jnp.exp(scores - top)
    total = jnp.sum(weights, axis=-1, keepdims=True)
    shares = (weights * (1.0 / total)).astype(BF)
    mixed_ref[...] = matmul(shares, v_ref[...]).astype(BF)
    logsum_ref[0] = top + jnp.log(total)


def backward_kernel(
    q_ref, k_ref, v_ref, g_ref, lo_ref, hi_ref, logsum_ref, dq_ref, dk_ref, dv_ref, dk_sum, dv_sum
):
    member = lax.rem(pl.program_id(0), GROUP)
    queries, keys, grads = q_ref[...], k_ref[...], g_ref[...]
    scores = against(queries, keys) * FACTOR
    allowed = allowed_of(lo_ref, hi_ref, *scores.shape)
    shares = jnp.where(allowed, jnp.exp(jnp.where(allowed, scores, NEGATIVE) - logsum_ref[0]), 0.0)
    grad_shares = against(grads, v_ref[...])
    delta = jnp.sum(shares * grad_shares, axis=-1, keepdims=True)
    grad_scores = (shares * (grad_shares - delta)).astype(BF)
    dq_ref[...] = matmul(grad_scores, keys) * FACTOR
    dk = outer(grad_scores, queries) * FACTOR
    dv = outer(shares.astype(BF), grads)

    @pl.when(member == 0)
    def _():
        dk_sum[...] = dk
        dv_sum[...] = dv

    @pl.when(member > 0)
    def _():
        dk_sum[...] += dk
        dv_sum[...] += dv

    @pl.when(member == GROUP - 1)
    def _():
        dk_ref[...] = dk_sum[...].astype(BF)
        dv_ref[...] = dv_sum[...].astype(BF)


def attention_forward(queries, keys, values, lo, hi):
    rows, length = queries.shape[0], keys.shape[0]
    head = pl.BlockSpec((rows, HEAD_DIM), lambda h: (0, h))
    kv = pl.BlockSpec((length, HEAD_DIM), lambda h: (0, h // GROUP))
    column = pl.BlockSpec((rows, 1), lambda h: (0, 0))
    stat = pl.BlockSpec((1, rows, 1), lambda h: (h, 0, 0))
    return pl.pallas_call(
        forward_kernel,
        grid=(HEADS,),
        in_specs=[head, kv, kv, column, column],
        out_specs=[head, stat],
        out_shape=[
            jax.ShapeDtypeStruct((rows, WIDTH), BF),
            jax.ShapeDtypeStruct((HEADS, rows, 1), F32),
        ],
        compiler_params=pltpu.CompilerParams(vmem_limit_bytes=VMEM_LIMIT),
        cost_estimate=pl.CostEstimate(
            flops=4 * rows * length * WIDTH,
            bytes_accessed=4 * length * KV_WIDTH + 4 * rows * WIDTH,
            transcendentals=rows * length * HEADS,
        ),
        name="attention_forward",
    )(queries, keys, values, lo, hi)


def attention_backward(queries, keys, values, grads, lo, hi, logsum):
    rows, length = queries.shape[0], keys.shape[0]
    head = pl.BlockSpec((rows, HEAD_DIM), lambda h: (0, h))
    kv = pl.BlockSpec((length, HEAD_DIM), lambda h: (0, h // GROUP))
    column = pl.BlockSpec((rows, 1), lambda h: (0, 0))
    stat = pl.BlockSpec((1, rows, 1), lambda h: (h, 0, 0))
    return pl.pallas_call(
        backward_kernel,
        grid=(HEADS,),
        in_specs=[head, kv, kv, head, column, column, stat],
        out_specs=[head, kv, kv],
        out_shape=[
            jax.ShapeDtypeStruct((rows, WIDTH), F32),
            jax.ShapeDtypeStruct((length, KV_WIDTH), BF),
            jax.ShapeDtypeStruct((length, KV_WIDTH), BF),
        ],
        scratch_shapes=[pltpu.VMEM((length, HEAD_DIM), F32), pltpu.VMEM((length, HEAD_DIM), F32)],
        compiler_params=pltpu.CompilerParams(vmem_limit_bytes=VMEM_LIMIT),
        cost_estimate=pl.CostEstimate(
            flops=10 * rows * length * WIDTH,
            bytes_accessed=8 * length * KV_WIDTH + 8 * rows * WIDTH,
            transcendentals=rows * length * HEADS,
        ),
        name="attention_backward",
    )(queries, keys, values, grads, lo, hi, logsum)


def gather(value, axis):
    return lax.all_gather(value, axis, axis=0, tiled=True)


def scatter_sum(value, axis):
    return lax.psum_scatter(value, axis, scatter_dimension=0, tiled=True)


def swap(value, axis):
    return lax.all_to_all(value, axis, 0, 0, tiled=True)


def body(
    tokens,
    segments,
    w_query,
    b_query,
    w_key,
    b_key,
    w_value,
    b_value,
    w_out,
    norm_attn,
    w_gate,
    w_up,
    w_down,
    norm_mlp,
    cotangent,
    *,
    seq,
    ctx,
):
    rows = tokens.shape[0]
    devices = seq * ctx
    share = w_query.shape[0]
    vshare = b_value.shape[0]
    ident = segments[0]
    length = ident.shape[0]
    offset = lax.axis_index("ctx") * rows
    hi = offset + jnp.arange(rows, dtype=jnp.int32)
    lo = lax.dynamic_slice_in_dim(ident, offset, rows)
    cosine_all, sine_all = rope_tables(jnp.arange(length, dtype=jnp.int32) - ident)
    cosine = lax.dynamic_slice_in_dim(cosine_all, offset, rows)
    sine = lax.dynamic_slice_in_dim(sine_all, offset, rows)
    hi, lo = hi[:, None], lo[:, None]

    small = jnp.stack([norm_attn, norm_mlp, b_query, jnp.pad(b_value, (0, share - vshare))], axis=1)
    small = jnp.pad(small, ((0, 0), (0, 124)))
    proj = gather(jnp.concatenate([w_query, w_key, w_value, small], axis=1), ALL)
    qkv_weight = proj[:, :QKV]
    vectors = proj[:, QKV:QKV + 4].astype(F32).T
    attn_gain, mlp_gain, query_bias = vectors[0][None], vectors[1][None], vectors[2][None]
    value_bias = vectors[3].reshape(devices, share)[:, :vshare].reshape(1, KV_WIDTH)
    tokens_all = gather(tokens, "ctx")
    out_weight = gather(w_out, ALL)

    hidden_share = w_down.shape[0]
    chunk = seq * hidden_share

    def to_columns(weight):
        parts = weight.reshape(share, seq, ctx, hidden_share).transpose(2, 0, 1, 3)
        return parts.reshape(ctx * share, chunk)

    gate_weight = gather(swap(to_columns(w_gate), "ctx"), "seq")
    up_weight = gather(swap(to_columns(w_up), "ctx"), "seq")
    down_weight = gather(w_down, "seq")
    cotangent_all = gather(cotangent, "ctx")

    inputs = tokens.astype(F32)
    scale_attn = inverse_rms(inputs)
    normed = (inputs * scale_attn * attn_gain).astype(BF)
    inputs_all = tokens_all.astype(F32)
    normed_all = (inputs_all * inverse_rms(inputs_all) * attn_gain).astype(BF)
    query_pre = matmul(normed, qkv_weight[:, :WIDTH]) + query_bias
    key_value = matmul(normed_all, qkv_weight[:, WIDTH:])
    queries = rotate(query_pre, cosine, sine, 1.0).astype(BF)
    keys = rotate(key_value[:, :KV_WIDTH] + b_key.astype(F32)[None], cosine_all, sine_all, 1.0).astype(BF)
    values = (key_value[:, KV_WIDTH:] + value_bias).astype(BF)
    mixed, logsum = attention_forward(queries, keys, values, lo, hi)
    middle = inputs + matmul(mixed, out_weight)

    scale_mlp = inverse_rms(middle)
    normed_mlp = gather((middle * scale_mlp * mlp_gain).astype(BF), "ctx")
    gate = matmul(normed_mlp, gate_weight)
    upper = matmul(normed_mlp, up_weight)
    grad_hidden = against(cotangent_all, down_weight)
    logistic = jax.nn.sigmoid(gate)
    hidden = (gate * logistic * upper).astype(BF)
    grad_gate = (grad_hidden * upper * logistic * (1.0 + gate * (1.0 - logistic))).astype(BF)
    grad_upper = (grad_hidden * gate * logistic).astype(BF)
    back = against(grad_gate, gate_weight) + against(grad_upper, up_weight)
    grad_normed_mlp = scatter_sum(back.astype(BF), "ctx").astype(F32)
    output = middle + scatter_sum(matmul(hidden, down_weight).astype(BF), "ctx").astype(F32)

    grad_w_down = scatter_sum(outer(hidden, cotangent_all).astype(BF), "seq").astype(F32)

    def from_columns(grad):
        parts = swap(scatter_sum(grad.astype(BF), "seq"), "ctx").astype(F32)
        parts = parts.reshape(ctx, share, seq, hidden_share).transpose(1, 2, 0, 3)
        return parts.reshape(share, devices * hidden_share)

    grad_w_gate = from_columns(outer(normed_mlp, grad_gate))
    grad_w_up = from_columns(outer(normed_mlp, grad_upper))

    cotangent_wide = cotangent.astype(F32)
    grad_norm_mlp = jnp.sum(grad_normed_mlp * middle * scale_mlp, axis=0)
    weighted_mlp = grad_normed_mlp * mlp_gain
    grad_middle = (
        cotangent_wide
        + scale_mlp * weighted_mlp
        - middle * (scale_mlp * scale_mlp * scale_mlp) * jnp.mean(weighted_mlp * middle, axis=-1, keepdims=True)
    )

    grad_branch = grad_middle.astype(BF)
    grad_mixed = against(grad_branch, out_weight).astype(BF)
    grad_w_out = scatter_sum(outer(mixed, grad_branch).astype(BF), ALL).astype(F32)
    dq, dk, dv = attention_backward(queries, keys, values, grad_mixed, lo, hi, logsum)
    terms = swap(jnp.concatenate([dk, dv], axis=1), "ctx").reshape(ctx, rows, 2 * KV_WIDTH)
    terms = jnp.sum(terms.astype(F32), axis=0)
    grad_query = rotate(dq, cosine, sine, -1.0).astype(BF)
    grad_key = rotate(terms[:, :KV_WIDTH], cosine, sine, -1.0).astype(BF)
    grad_value = terms[:, KV_WIDTH:].astype(BF)
    grad_qkv = jnp.concatenate([grad_query, grad_key, grad_value], axis=1)

    columns = QKV // ctx
    turned = grad_qkv.reshape(rows, ctx, columns).transpose(1, 0, 2).reshape(ctx * rows, columns)
    grad_w_qkv = outer(normed_all, swap(turned, "ctx"))
    grad_w_qkv = swap(scatter_sum(grad_w_qkv.astype(BF), "seq"), "ctx").astype(F32)
    grad_w_qkv = grad_w_qkv.reshape(ctx, share, columns).transpose(1, 0, 2).reshape(share, QKV)

    grad_normed = against(grad_qkv, qkv_weight)
    grad_norm_attn = jnp.sum(grad_normed * inputs * scale_attn, axis=0)
    weighted_attn = grad_normed * attn_gain
    grad_tokens = (
        grad_middle
        + scale_attn * weighted_attn
        - inputs * (scale_attn * scale_attn * scale_attn) * jnp.mean(weighted_attn * inputs, axis=-1, keepdims=True)
    )

    bias = jnp.sum(grad_qkv.astype(F32), axis=0)
    parts = jnp.concatenate(
        [
            grad_norm_attn.reshape(devices, share),
            grad_norm_mlp.reshape(devices, share),
            bias[:WIDTH].reshape(devices, share),
            bias[WIDTH + KV_WIDTH:].reshape(devices, vshare),
            jnp.broadcast_to(bias[None, WIDTH:WIDTH + KV_WIDTH], (devices, KV_WIDTH)),
        ],
        axis=1,
    )
    sums = jnp.sum(swap(parts, ALL), axis=0)
    g_norm_attn, g_norm_mlp, g_b_query, g_b_value, g_b_key = jnp.split(
        sums, [share, 2 * share, 3 * share, 3 * share + vshare]
    )
    return (
        output,
        grad_tokens,
        grad_w_qkv[:, :WIDTH],
        g_b_query,
        grad_w_qkv[:, WIDTH:WIDTH + KV_WIDTH],
        g_b_key,
        grad_w_qkv[:, WIDTH + KV_WIDTH:],
        g_b_value,
        grad_w_out,
        g_norm_attn,
        grad_w_gate,
        grad_w_up,
        grad_w_down,
        g_norm_mlp,
    )


def solution(mesh):
    rows2, rows1 = P(ALL, None), P(ALL)
    return jax.shard_map(
        functools.partial(body, seq=mesh.shape["seq"], ctx=mesh.shape["ctx"]),
        mesh=mesh,
        in_specs=(
            rows2,
            P("seq", None),
            rows2,
            rows1,
            rows2,
            P(),
            rows2,
            rows1,
            rows2,
            rows1,
            rows2,
            rows2,
            rows2,
            rows1,
            rows2,
        ),
        out_specs=(
            rows2,
            rows2,
            rows2,
            rows1,
            rows2,
            P(),
            rows2,
            rows1,
            rows2,
            rows1,
            rows2,
            rows2,
            rows2,
            rows1,
        ),
        check_vma=False,
    )
```

```python
import functools
import math

import jax
import jax.numpy as jnp
from jax import lax
from jax.experimental import pallas as pl
from jax.experimental.pallas import tpu as pltpu
from jax.sharding import Mesh
from jax.sharding import PartitionSpec as P

HEADS = 12
KV_HEADS = 2
HEAD_DIM = 128
WIDTH = 1536
KV_WIDTH = 256
GROUP = HEADS // KV_HEADS
QKV = WIDTH + 2 * KV_WIDTH
LANES = 128

EPS = 1e-06
THETA = 1000000.0
NEGATIVE = -1e30
FACTOR = HEAD_DIM ** (-0.5)
VMEM_LIMIT = 58 * 1024 * 1024

CTX = ("z", "y")
ALL = ("seq", "z", "y")
BF = jnp.bfloat16
F32 = jnp.float32
LEFT = 1024
VMEM = pl.BlockSpec(memory_space=pltpu.VMEM)
SMEM = pl.BlockSpec(memory_space=pltpu.SMEM)


def shape(dims, kind):
    return jax.ShapeDtypeStruct(dims, kind)


def cost(flops, nbytes, exps=0):
    return pl.CostEstimate(flops=int(flops), bytes_accessed=int(nbytes), transcendentals=int(exps))


def whole(value):
    return pl.BlockSpec(value.shape, lambda i: (0,) * value.ndim)


def params():
    return pltpu.CompilerParams(vmem_limit_bytes=VMEM_LIMIT)


def inverse_rms(values):
    return lax.rsqrt(jnp.mean(values * values, axis=-1, keepdims=True) + EPS)


def matmul(left, right):
    return jnp.dot(left, right, preferred_element_type=F32)


def against(left, weight):
    return lax.dot_general(left, weight, (((1,), (1,)), ((), ())), preferred_element_type=F32)


def outer(left, right):
    return lax.dot_general(left, right, (((0,), (0,)), ((), ())), preferred_element_type=F32)


def rope_tables(positions):
    half = HEAD_DIM // 2
    freqs = THETA ** (-(2.0 * jnp.arange(half, dtype=F32)) / HEAD_DIM)
    angles = positions.astype(F32)[:, None] * freqs[None, :]
    cosine, sine = jnp.cos(angles), jnp.sin(angles)
    return jnp.concatenate([cosine, cosine], axis=-1), jnp.concatenate([-sine, sine], axis=-1)


def rotate(head, cosine, sine):
    return head * cosine + pltpu.roll(head, HEAD_DIM // 2, 1) * sine


def rotate_back(head, cosine, sine):
    return head * cosine - pltpu.roll(head, HEAD_DIM // 2, 1) * sine


def columns_out_kernel(gate_ref, up_ref, out_ref, *, seq, ctx, run, padded):
    chunk = seq * padded
    rows = gate_ref.shape[0]
    blank = jnp.zeros((rows, padded - run), BF)
    for which, ref in enumerate((gate_ref, up_ref)):
        for part in range(ctx):
            pieces = []
            for place in range(seq):
                start = (place * ctx + part) * run
                pieces += [ref[:, start:start + run], blank]
            out_ref[part, :, which * chunk:(which + 1) * chunk] = jnp.concatenate(pieces, axis=1)


def columns_out(gate, up, seq, ctx, run, padded):
    rows = gate.shape[0]
    return pl.pallas_call(
        functools.partial(columns_out_kernel, seq=seq, ctx=ctx, run=run, padded=padded),
        in_specs=[VMEM, VMEM],
        out_specs=VMEM,
        out_shape=shape((ctx, rows, 2 * seq * padded), BF),
        compiler_params=params(),
        cost_estimate=cost(0, 4 * gate.size * 2),
        name="columns_out",
    )(gate, up)


def columns_in_kernel(gate_in_ref, up_in_ref, gate_ref, up_ref, *, seq, ctx, run, padded):
    for in_ref, ref in ((gate_in_ref, gate_ref), (up_in_ref, up_ref)):
        pieces = []
        for place in range(seq):
            for part in range(ctx):
                pieces.append(in_ref[part, :, place * padded:place * padded + run])
        ref[...] = jnp.concatenate(pieces, axis=1).astype(F32)


def columns_in(gate, up, seq, ctx, run, padded):
    rows = gate.shape[1]
    return pl.pallas_call(
        functools.partial(columns_in_kernel, seq=seq, ctx=ctx, run=run, padded=padded),
        in_specs=[VMEM, VMEM],
        out_specs=[VMEM, VMEM],
        out_shape=[shape((rows, seq * ctx * run), F32)] * 2,
        compiler_params=params(),
        cost_estimate=cost(0, gate.size * 12),
        name="columns_in",
    )(gate, up)


def runs_of(core, own_ref, other_ref):
    run = own_ref.shape[0] // 2
    for x in range(2):
        for flip, ref in enumerate((own_ref, other_ref)):
            start = pl.multiple_of((2 * x + (core ^ flip)) * run, LANES)
            yield pl.ds(start, run), ref, slice(x * run, (x + 1) * run)


def times(core, left_ref, own_ref, other_ref, width):
    total = None
    for lanes, ref, rows in runs_of(core, own_ref, other_ref):
        term = matmul(left_ref[:, lanes], ref[rows, :width])
        total = term if total is None else total + term
    return total


def project_kernel(
    core_ref, tokens_ref, left_ref, left_other_ref, right_ref, right_other_ref,
    gain_ref, qbias_ref, kbias_ref, vbias_ref, cos_ref, sin_ref,
    normed_ref, query_ref, pair_out_ref,
):
    core = core_ref[0]
    inputs = tokens_ref[...].astype(F32)
    normed_ref[...] = (inputs * inverse_rms(inputs) * gain_ref[...]).astype(BF)
    left = times(core, normed_ref, left_ref, left_other_ref, LEFT)
    right = times(core, normed_ref, right_ref, right_other_ref, QKV - LEFT)
    query = jnp.concatenate([left, right[:, :WIDTH - LEFT]], axis=1) + qbias_ref[...]
    pair = right[:, WIDTH - LEFT:]
    key = pair[:, :KV_WIDTH] + kbias_ref[...]
    cosine, sine = cos_ref[...], sin_ref[...]
    for h in range(HEADS):
        lanes = slice(h * HEAD_DIM, (h + 1) * HEAD_DIM)
        query_ref[:, lanes] = rotate(query[:, lanes], cosine, sine).astype(BF)
    for g in range(KV_HEADS):
        lanes = slice(g * HEAD_DIM, (g + 1) * HEAD_DIM)
        pair_out_ref[:, lanes] = rotate(key[:, lanes], cosine, sine).astype(BF)
    pair_out_ref[:, KV_WIDTH:] = (pair[:, KV_WIDTH:] + vbias_ref[...]).astype(BF)


def project(core, tokens, left, right, gain, qbias, kbias, vbias, cosine, sine):
    rows = tokens.shape[0]
    return pl.pallas_call(
        project_kernel,
        in_specs=[SMEM] + [VMEM] * 11,
        out_specs=[VMEM] * 3,
        out_shape=[shape((rows, WIDTH), BF), shape((rows, WIDTH), BF), shape((rows, 2 * KV_WIDTH), BF)],
        compiler_params=params(),
        cost_estimate=cost(2 * rows * WIDTH * QKV, 2 * WIDTH * QKV + 6 * rows * WIDTH),
        name="project",
    )(core, tokens, *left, *right, gain, qbias, kbias, vbias, cosine, sine)


def vectors_kernel(core_ref, own_ref, other_ref, out_ref):
    for lanes, ref, rows in runs_of(core_ref[0], own_ref, other_ref):
        out_ref[:, lanes] = ref[rows, :].astype(F32).T[:out_ref.shape[0]]


def vectors_of(core, right, count):
    depth, width = right[0].shape
    block = pl.BlockSpec((depth, LANES), lambda i: (0, width // LANES - 1))
    return pl.pallas_call(
        vectors_kernel,
        grid=(1,),
        in_specs=[SMEM, block, block],
        out_specs=pl.BlockSpec((count, 2 * depth), lambda i: (0, 0)),
        out_shape=shape((count, 2 * depth), F32),
        compiler_params=params(),
        cost_estimate=cost(0, 4 * depth * LANES),
        name="vectors",
    )(core, *right)


def allowed_of(lo_ref, hi_ref, rows, length):
    places = lax.broadcasted_iota(jnp.int32, (rows, length), 1)
    return (places >= lo_ref[...]) & (places <= hi_ref[...])


def forward_kernel(q_ref, k_ref, v_ref, lo_ref, hi_ref, mixed_ref, logsum_ref):
    scores = against(q_ref[...], k_ref[...]) * FACTOR
    allowed = allowed_of(lo_ref, hi_ref, *scores.shape)
    scores = jnp.where(allowed, scores, NEGATIVE)
    top = jnp.max(scores, axis=-1, keepdims=True)
    weights = jnp.exp(scores - top)
    total = jnp.sum(weights, axis=-1, keepdims=True)
    shares = (weights * (1.0 / total)).astype(BF)
    mixed_ref[...] = matmul(shares, v_ref[...]).astype(BF)
    logsum_ref[0] = top + jnp.log(total)


def attention_forward(queries, pair, lo, hi):
    rows, length = queries.shape[0], pair.shape[0]
    head = pl.BlockSpec((rows, HEAD_DIM), lambda h: (0, h))
    key = pl.BlockSpec((length, HEAD_DIM), lambda h: (0, h // GROUP))
    value = pl.BlockSpec((length, HEAD_DIM), lambda h: (0, KV_HEADS + h // GROUP))
    column = pl.BlockSpec((rows, 1), lambda h: (0, 0))
    stat = pl.BlockSpec((1, rows, 1), lambda h: (h, 0, 0))
    return pl.pallas_call(
        forward_kernel,
        grid=(HEADS,),
        in_specs=[head, key, value, column, column],
        out_specs=[head, stat],
        out_shape=[shape((rows, WIDTH), BF), shape((HEADS, rows, 1), F32)],
        compiler_params=params(),
        cost_estimate=cost(4 * rows * length * WIDTH, 4 * length * KV_WIDTH + 4 * rows * WIDTH, rows * length * HEADS),
        name="attention_forward",
    )(queries, pair, pair, lo, hi)


def backward_kernel(
    core_ref, q_ref, k_ref, v_ref, g_ref, lo_ref, hi_ref, logsum_ref, cos_ref, sin_ref, cosq_ref, sinq_ref,
    normed_ref, mixed_ref, branch_ref, dq_ref, dkv_ref, keep_ref, send_ref, dk_sum, dv_sum, turned_ref,
):
    head = pl.program_id(0)

    @pl.when(head == 0)
    def _():
        turned_ref[...] = normed_ref[...].astype(F32).T.astype(BF)

    group = head // GROUP
    member = lax.rem(head, GROUP)
    queries, keys, grads = q_ref[...], k_ref[...], g_ref[...]
    scores = against(queries, keys) * FACTOR
    allowed = allowed_of(lo_ref, hi_ref, *scores.shape)
    shares = jnp.where(allowed, jnp.exp(jnp.where(allowed, scores, NEGATIVE) - logsum_ref[0]), 0.0)
    grad_shares = against(grads, v_ref[...])
    delta = jnp.sum(shares * grad_shares, axis=-1, keepdims=True)
    grad_scores = (shares * (grad_shares - delta)).astype(BF)
    dq = matmul(grad_scores, keys) * FACTOR
    dq = rotate_back(dq, cosq_ref[...], sinq_ref[...]).astype(BF)
    dq_ref[...] = dq
    dk = outer(grad_scores, queries) * FACTOR
    dv = outer(shares.astype(BF), grads)

    @pl.when(member == 0)
    def _():
        dk_sum[...] = dk
        dv_sum[...] = dv

    @pl.when(member > 0)
    def _():
        dk_sum[...] += dk
        dv_sum[...] += dv

    @pl.when(member == GROUP - 1)
    def _():
        here = pl.multiple_of(group * HEAD_DIM, HEAD_DIM)
        there = pl.multiple_of(KV_WIDTH + group * HEAD_DIM, HEAD_DIM)
        dkv_ref[:, pl.ds(here, HEAD_DIM)] = rotate_back(dk_sum[...], cos_ref[...], sin_ref[...]).astype(BF)
        dkv_ref[:, pl.ds(there, HEAD_DIM)] = dv_sum[...].astype(BF)

    core = core_ref[0]
    columns = pl.ds(pl.multiple_of(head * HEAD_DIM, HEAD_DIM), HEAD_DIM)
    for lanes, ref, rows in runs_of(core, keep_ref, send_ref):
        ref[rows, columns] = matmul(turned_ref[lanes, :], dq).astype(BF)
    run = keep_ref.shape[0] // 2
    heads = run // HEAD_DIM
    place = head // heads
    row = pl.multiple_of(place // 2 * run + lax.rem(head, heads) * HEAD_DIM, HEAD_DIM)
    terms = outer(mixed_ref[...], branch_ref[...]).astype(BF)
    mine = lax.rem(place, 2) == core

    @pl.when(mine)
    def _():
        keep_ref[pl.ds(row, HEAD_DIM), WIDTH:] = terms

    @pl.when(jnp.logical_not(mine))
    def _():
        send_ref[pl.ds(row, HEAD_DIM), WIDTH:] = terms


def attention_backward(
    core, queries, pair, grads, lo, hi, logsum, cosine, sine, cosine_own, sine_own, normed, mixed, grad_branch
):
    rows, length = queries.shape[0], pair.shape[0]
    once = pl.Buffered(1)
    head = pl.BlockSpec((rows, HEAD_DIM), lambda h: (0, h))
    key = pl.BlockSpec((length, HEAD_DIM), lambda h: (0, h // GROUP))
    value = pl.BlockSpec((length, HEAD_DIM), lambda h: (0, KV_HEADS + h // GROUP))
    column = pl.BlockSpec((rows, 1), lambda h: (0, 0))
    stat = pl.BlockSpec((1, rows, 1), lambda h: (h, 0, 0))
    fixed = lambda x: pl.BlockSpec(x.shape, lambda h: (0, 0), pipeline_mode=once)
    terms = shape((WIDTH // 2, 2 * WIDTH), BF)
    return pl.pallas_call(
        backward_kernel,
        grid=(HEADS,),
        in_specs=[SMEM, head, key, value, head, column, column, stat]
        + [fixed(x) for x in (cosine, sine, cosine_own, sine_own, normed)]
        + [head, fixed(grad_branch)],
        out_specs=[head, pl.BlockSpec((length, 2 * KV_WIDTH), lambda h: (0, 0))]
        + [pl.BlockSpec(terms.shape, lambda h: (0, 0))] * 2,
        out_shape=[shape((rows, WIDTH), BF), shape((length, 2 * KV_WIDTH), BF), terms, terms],
        scratch_shapes=[
            pltpu.VMEM((length, HEAD_DIM), F32),
            pltpu.VMEM((length, HEAD_DIM), F32),
            pltpu.VMEM((WIDTH, rows), BF),
        ],
        compiler_params=params(),
        cost_estimate=cost(10 * rows * length * WIDTH, 16 * length * KV_WIDTH, rows * length * HEADS),
        name="attention_backward",
    )(core, queries, pair, pair, grads, lo, hi, logsum, cosine, sine, cosine_own, sine_own, normed, mixed, grad_branch)


def branch_kernel(core_ref, mixed_ref, *refs):
    weights, (tokens_ref, gain_ref, middle_ref, normed_ref) = refs[:4], refs[4:]
    width = weights[0].shape[1]
    parts = [times(core_ref[0], mixed_ref, weights[2 * i], weights[2 * i + 1], width) for i in range(2)]
    middle = tokens_ref[...].astype(F32) + jnp.concatenate(parts, axis=1)
    middle_ref[...] = middle
    normed_ref[...] = (middle * inverse_rms(middle) * gain_ref[...]).astype(BF)


def branch(core, mixed, out_weight, tokens, gain):
    rows = mixed.shape[0]
    return pl.pallas_call(
        branch_kernel,
        in_specs=[SMEM] + [VMEM] * 7,
        out_specs=[VMEM] * 2,
        out_shape=[shape((rows, WIDTH), F32), shape((rows, WIDTH), BF)],
        compiler_params=params(),
        cost_estimate=cost(2 * rows * WIDTH * WIDTH, 2 * WIDTH * WIDTH),
        name="branch",
    )(core, mixed, *out_weight, tokens, gain)


def mlp_kernel(
    near_ref, other_ref, cot_near_ref, cot_other_ref, gate_ref, up_ref, down_ref,
    hidden_ref, grad_gate_ref, grad_up_ref, back_ref, forth_ref,
):
    tokens = jnp.concatenate([near_ref[...], other_ref[...]], axis=0)
    cotangent = jnp.concatenate([cot_near_ref[...], cot_other_ref[...]], axis=0)
    gate = matmul(tokens, gate_ref[...])
    upper = matmul(tokens, up_ref[...])
    grad_hidden = against(cotangent, down_ref[...])
    logistic = 1.0 / (1.0 + jnp.exp(-gate))
    silu = gate * logistic
    hidden = (silu * upper).astype(BF)
    hidden_ref[...] = hidden
    grad_gate = (grad_hidden * upper * logistic * (1.0 + gate * (1.0 - logistic))).astype(BF)
    grad_upper = (grad_hidden * silu).astype(BF)
    grad_gate_ref[...] = grad_gate
    grad_up_ref[...] = grad_upper
    back_ref[...] = (against(grad_gate, gate_ref[...]) + against(grad_upper, up_ref[...])).astype(BF)
    forth_ref[...] = matmul(hidden, down_ref[...]).astype(BF)


def mlp(near, other, cot_near, cot_other, gate_up, down):
    rows = 2 * near.shape[0]
    chunk = down.shape[0]
    part = lambda n: pl.BlockSpec((WIDTH, chunk), lambda i: (0, n))
    made = [shape((rows, width), BF) for width in (chunk, chunk, chunk, WIDTH, WIDTH)]
    return pl.pallas_call(
        mlp_kernel,
        grid=(1,),
        in_specs=[whole(near)] * 4 + [part(0), part(1), whole(down)],
        out_specs=[whole(x) for x in made],
        out_shape=made,
        compiler_params=params(),
        cost_estimate=cost(12 * rows * WIDTH * chunk, 6 * WIDTH * chunk + 14 * rows * WIDTH, rows * chunk),
        name="mlp",
    )(near, other, cot_near, cot_other, gate_up, gate_up, down)


def outer_kernel(*refs, counts):
    blocks, position = [], 0
    for count in counts:
        blocks.append(jnp.concatenate([ref[...] for ref in refs[position:position + count]], axis=0))
        position += count
    for right, out_ref in zip(blocks[1:], refs[position:]):
        out_ref[...] = outer(blocks[0], right).astype(BF)


def outer_blocks(lefts, rights, name):
    depth = sum(x.shape[0] for x in lefts)
    width = lefts[0].shape[1]
    across = [blocks[0].shape[1] for blocks in rights]
    tile = 384 if width % 384 == 0 else width
    flat = [x for blocks in rights for x in blocks]
    return pl.pallas_call(
        functools.partial(outer_kernel, counts=(len(lefts), *map(len, rights))),
        grid=(width // tile,),
        in_specs=[pl.BlockSpec((x.shape[0], tile), lambda i: (0, i)) for x in lefts]
        + [pl.BlockSpec(x.shape, lambda i: (0, 0), pipeline_mode=pl.Buffered(1)) for x in flat],
        out_specs=[pl.BlockSpec((tile, n), lambda i: (i, 0)) for n in across],
        out_shape=[shape((width, n), BF) for n in across],
        compiler_params=params(),
        cost_estimate=cost(2 * depth * width * sum(across), 2 * (depth + width) * (width + sum(across))),
        name=name,
    )(*lefts, *flat)


def middle_kernel(
    core_ref, first_ref, middle_ref, cotangent_ref, gain_ref, *refs
):
    weights, second, (grad_ref, branch_ref, mixed_ref, norm_ref) = refs[:4], refs[4:-4], refs[-4:]
    total = jnp.concatenate(
        [jnp.sum(first_ref[...].astype(F32), axis=0), sum(ref[...].astype(F32) for ref in second)], axis=0
    )
    middle = middle_ref[...]
    scale = inverse_rms(middle)
    norm_ref[...] = jnp.sum(total * middle * scale, axis=0, keepdims=True)
    weighted = total * gain_ref[...]
    grad = (
        cotangent_ref[...].astype(F32)
        + scale * weighted
        - middle * (scale * scale * scale) * jnp.mean(weighted * middle, axis=-1, keepdims=True)
    )
    grad_ref[...] = grad
    low = grad.astype(BF)
    branch_ref[...] = low
    width = weights[0].shape[1]
    core = core_ref[0]
    for first, second in zip(runs_of(core, *weights[:2]), runs_of(core, *weights[2:])):
        lanes, ref, rows = first
        mixed_ref[:, lanes] = (
            against(low[:, :width], ref[rows, :]) + against(low[:, width:], second[1][rows, :])
        ).astype(BF)


def middle_back(core, terms, middle, cotangent, gain, out_weight):
    rows = middle.shape[0]
    return pl.pallas_call(
        middle_kernel,
        in_specs=[SMEM] + [VMEM] * (8 + len(terms[1])),
        out_specs=[VMEM] * 4,
        out_shape=[shape((rows, WIDTH), F32), shape((rows, WIDTH), BF), shape((rows, WIDTH), BF), shape((1, WIDTH), F32)],
        compiler_params=params(),
        cost_estimate=cost(2 * rows * WIDTH * WIDTH, 2 * WIDTH * WIDTH + 20 * rows * WIDTH),
        name="middle_back",
    )(core, terms[0], middle, cotangent, gain, *out_weight, *terms[1])


def tokens_kernel(
    core_ref, grads_ref, left_ref, left_other_ref, right_ref, right_other_ref, tokens_ref, gain_ref, middle_ref,
    out_ref, norm_ref, bias_ref, total_ref,
):
    grads = grads_ref[...]
    bias_ref[...] = jnp.sum(grads.astype(F32), axis=0, keepdims=True)
    core = core_ref[0]
    for first, second in zip(runs_of(core, left_ref, left_other_ref), runs_of(core, right_ref, right_other_ref)):
        lanes, ref, rows = first
        total_ref[:, lanes] = against(grads[:, :LEFT], ref[rows, :]) + against(
            grads[:, LEFT:], second[1][rows, :QKV - LEFT]
        )
    grad_normed = total_ref[...]
    inputs = tokens_ref[...].astype(F32)
    scale = inverse_rms(inputs)
    norm_ref[...] = jnp.sum(grad_normed * inputs * scale, axis=0, keepdims=True)
    weighted = grad_normed * gain_ref[...]
    out_ref[...] = (
        middle_ref[...]
        + scale * weighted
        - inputs * (scale * scale * scale) * jnp.mean(weighted * inputs, axis=-1, keepdims=True)
    )


def tokens_back(core, grads, left, right, tokens, gain, middle):
    rows = tokens.shape[0]
    return pl.pallas_call(
        tokens_kernel,
        in_specs=[SMEM] + [VMEM] * 8,
        out_specs=[VMEM] * 3,
        out_shape=[shape((rows, WIDTH), F32), shape((1, WIDTH), F32), shape((1, QKV), F32)],
        scratch_shapes=[pltpu.VMEM((rows, WIDTH), F32)],
        compiler_params=params(),
        cost_estimate=cost(2 * rows * WIDTH * QKV, 2 * WIDTH * QKV + 12 * rows * WIDTH),
        name="tokens_back",
    )(core, grads, *left, *right, tokens, gain, middle)


def gather(value, axis):
    return lax.all_gather(value, axis, axis=0, tiled=True)


def scatter_sum(value, axis):
    return lax.psum_scatter(value, axis, scatter_dimension=0, tiled=True)


def swap(value, axis):
    return lax.all_to_all(value, axis, 0, 0, tiled=True)


def hop(value, axis, size=2, flip=1):
    return lax.ppermute(value, axis, [(i, i ^ flip) for i in range(size)])


def after(value, *earlier):
    return lax.optimization_barrier((value, *earlier))[0]


def together(*values):
    return lax.optimization_barrier(values)


def gather_near(value, nz):
    copies = jnp.broadcast_to(value[None], (nz, *value.shape)).reshape(-1, value.shape[1])
    return swap(copies, "z").reshape(nz, *value.shape)


def add_low(left, right):
    return (left.astype(F32) + right.astype(F32)).astype(BF)


def exchange_near(blocks, nz, own_z):
    out = [lax.dynamic_index_in_dim(blocks, own_z, 0, keepdims=False)]
    for flip in range(1, nz):
        out.append(hop(lax.dynamic_index_in_dim(blocks, own_z ^ flip, 0, keepdims=False), "z", nz, flip))
    return out


def add_up(blocks):
    total = blocks[0].astype(F32)
    for block in blocks[1:]:
        total = total + block.astype(F32)
    return total


def pair(own, other, bit, axis):
    first, second = jnp.where(bit == 0, own, other), jnp.where(bit == 0, other, own)
    return jnp.stack([first, second], axis=axis)


def gather_z(value, nz, own_z):
    blocks = jnp.stack([value] + [hop(value, "z", nz, j) for j in range(1, nz)])
    return jnp.concatenate([lax.dynamic_slice_in_dim(blocks, own_z ^ j, 1) for j in range(nz)], axis=0)


def halve(value, axis, flip, size, bit, dim):
    keep = lax.dynamic_index_in_dim(value, bit, dim, keepdims=False)
    send = lax.dynamic_index_in_dim(value, 1 - bit, dim, keepdims=False)
    return add_low(keep, hop(send, axis, size, flip))


def sum_all(value, seq, nz):
    for axis, size in (("seq", seq), ("y", 2), ("z", nz)):
        flip = 1
        while flip < size:
            value = value + hop(value, axis, size, flip)
            flip *= 2
    return value


def body(
    tokens,
    segments,
    w_query,
    b_query,
    w_key,
    b_key,
    w_value,
    b_value,
    w_out,
    norm_attn,
    w_gate,
    w_up,
    w_down,
    norm_mlp,
    cotangent,
    *,
    seq,
    ctx,
):
    rows = tokens.shape[0]
    half = rows // 2
    nz = ctx // 2
    devices = seq * ctx
    share = w_query.shape[0]
    vshare = b_value.shape[0]
    run = w_down.shape[0]
    unit = LANES // math.gcd(LANES, seq)
    padded = -(-run // unit) * unit
    ident = segments[0]
    length = ident.shape[0]
    own_z, own_y, place = lax.axis_index("z"), lax.axis_index("y"), lax.axis_index("seq")
    index = 2 * own_z + own_y

    small = jnp.stack([norm_attn, norm_mlp, b_query, jnp.pad(b_value, (0, share - vshare))], axis=1)
    small = jnp.pad(small, ((0, 0), (0, LANES - 4)))
    projections = jnp.concatenate([w_query, w_key, w_value, small], axis=1)
    x, core = place // 2, place % 2
    over = lambda v, axis: hop(v, "seq", seq, 2) if axis == "x" else hop(v, "seq", seq, 1) if axis == "core" else hop(v, "y")
    flat = lambda v: v.reshape(2 * ctx * share, v.shape[-1])
    cuts = [slice(i * half, (i + 1) * half) for i in range(2)]
    count = nz * half
    cosine, sine = rope_tables(jnp.arange(length, dtype=jnp.int32) - ident)
    offset = index * rows
    hi = (offset + jnp.arange(rows, dtype=jnp.int32))[:, None]
    lo = lax.dynamic_slice_in_dim(ident, offset, rows)[:, None]
    tables = [cosine, sine] + [lax.dynamic_slice_in_dim(x, offset, rows) for x in (cosine, sine)] + [lo, hi]
    near = gather_near(projections, nz)
    turned = columns_out(w_gate, w_up, seq, ctx, run, padded).reshape(ctx * share, -1)
    turned = swap(after(turned, near), CTX)
    left, right = near[:, :, :LEFT], near[:, :, LEFT:]
    left_got, right_got, near, tables = together(
        over(left, "y"), over(right, "x"), gather_z(after(w_out, near), nz, own_z), tables
    )
    left, right = pair(left, left_got, own_y, 1), pair(right, right_got, x, 0)
    out_left, out_right = near[:, :, :WIDTH // 2], near[:, :, WIDTH // 2:]
    left_got, right_got, out_left_got, out_right_got = together(
        over(left, "x"), over(right, "y"), over(out_left, "y"), over(out_right, "x")
    )
    left, right = flat(pair(left, left_got, x, 0)), flat(pair(right, right_got, own_y, 2))
    out_left, out_right = pair(out_left, out_left_got, own_y, 1), pair(out_right, out_right_got, x, 0)
    left_got, right_got, out_left_got, out_right_got = together(
        over(left, "core"), over(right, "core"), over(out_left, "x"), over(out_right, "y")
    )
    left, right = (left, left_got), (right, right_got)
    out_left, out_right = flat(pair(out_left, out_left_got, x, 0)), flat(pair(out_right, out_right_got, own_y, 2))
    out_weight = (out_left, over(out_left, "core"), out_right, over(out_right, "core"))
    down = jnp.pad(w_down, ((0, padded - run), (0, 0)))
    down = gather(down, "seq")
    gate_up = gather(after(turned, left_got), "seq")
    cotangent_low = after(cotangent, turned)
    cot_near = [gather_near(cotangent_low[cuts[0]], nz).reshape(count, WIDTH)]
    cosine, sine, cosine_own, sine_own, lo, hi = tables
    core = core.astype(jnp.int32)[None]
    vectors = vectors_of(core, right, 8)
    attn_gain, mlp_gain, query_bias = vectors[0:1], vectors[1:2], vectors[2:3]
    value_bias = vectors[3].reshape(devices, share)[:, :vshare].reshape(1, KV_WIDTH)

    normed, queries, kv = project(
        core, tokens, left, right, attn_gain, query_bias, b_key.astype(F32)[None], value_bias, cosine_own, sine_own
    )
    near = gather_near(after(kv, cot_near[0]), nz)
    cot_near.append(gather_near(after(cotangent, near)[cuts[1]], nz).reshape(count, WIDTH))
    other = hop(near, "y")
    cot_other = [hop(after(x, other), "y") for x in cot_near]
    kv = pair(near, other, own_y, 1).reshape(length, 2 * KV_WIDTH)
    mixed, logsum = attention_forward(queries, kv, lo, hi)
    mixed, out_weight, cot_other[0] = together(mixed, out_weight, cot_other[0])
    middle, normed_mlp = branch(core, mixed, out_weight, tokens, mlp_gain)

    x_near = [gather_near(after(normed_mlp, cot_near[1])[cut], nz).reshape(count, WIDTH) for cut in cuts]
    x_other = [hop(x, "y") for x in x_near]
    runs = [mlp(x_near[0], x_other[0], cot_near[0], cot_other[0], gate_up, down)]
    x_other[1] = after(x_other[1], *runs[0])
    runs.append(mlp(x_near[1], x_other[1], cot_near[1], cot_other[1], gate_up, down))
    hidden, grads_gate, grads_up, back, forth = zip(*runs)
    sums = []
    for rows_back in back:
        sums.append(add_low(rows_back[:count], hop(after(rows_back[count:], *sums), "y")))
    far = [swap(sums[0], "z").reshape(nz, half, WIDTH), exchange_near(sums[1].reshape(nz, half, WIDTH), nz, own_z)]
    x_all = [x_near[0], x_other[0], x_near[1], x_other[1]]
    cots = [cot_near[0], cot_other[0], cot_near[1], cot_other[1]]
    forth_got = [hop(after(x[count:], *sums), "y") for x in forth]
    grads_gate, grads_up = after((grads_gate, grads_up), sums[1], far[0])
    hidden = after(hidden, forth_got[0])
    grad_w_gate, grad_w_up = outer_blocks(x_all, [grads_gate, grads_up], "gate_up_grads")
    grad_w_gate, grad_w_up = scatter_sum(grad_w_gate, "seq"), scatter_sum(grad_w_up, "seq")
    (grad_w_down,) = outer_blocks(hidden, [cots], "down_grads")
    grad_w_down = scatter_sum(grad_w_down, "seq")[:run].astype(F32)

    far, forth_got = together(far, forth_got)
    grad_middle, grad_branch, grad_mixed, norm_mlp_sum = middle_back(core, far, middle, cotangent, mlp_gain, out_weight)
    dq, dkv, keep, send = attention_backward(
        core, queries, kv, grad_mixed, lo, hi, logsum, cosine, sine, cosine_own, sine_own, normed, mixed, grad_branch
    )
    forth = jnp.concatenate(
        [add_low(x[:count], y).reshape(nz, half, WIDTH) for x, y in zip(forth, forth_got)], axis=1
    )
    forth = exchange_near(forth, nz, own_z)
    terms = swap(dkv, CTX).reshape(ctx, rows, 2 * KV_WIDTH)
    terms = jnp.sum(terms.astype(F32), axis=0).astype(BF)

    over_core = lambda v: halve(v, "seq", 1, seq, place % 2, 1)
    over_x = lambda v: halve(v, "seq", 2, seq, place // 2, 0)
    over_y = lambda v: halve(v, "y", 1, 2, own_y, v.ndim - 3)
    sides = add_low(keep, over(send, "core")).reshape(2, nz, 2, share, -1)
    grad_query, grad_out = over_x(sides[..., :WIDTH]), over_y(sides[..., WIDTH:])
    terms, sides_done = together(terms, sides[:1, :1, :1, :8, :LANES])
    grad_w_gate = swap(after(grad_w_gate, terms), CTX).reshape(ctx, share, -1)
    (grad_pair,) = outer_blocks([normed], [[terms]], "pair_grads")
    grad_tokens, norm_attn_sum, bias = tokens_back(
        core, jnp.concatenate([dq, after(terms, grad_pair)], axis=1), left, right, tokens, attn_gain, grad_middle
    )
    grad_pair, bias, forth, grad_out, grad_query = together(grad_pair, bias, forth, grad_out, grad_query)
    grad_pair = over_core(grad_pair.reshape(2, 2, nz, 2, share, -1))
    grad_out, grad_query = over_x(grad_out), over_y(grad_query)
    grad_w_gate, grad_out, grad_query, grad_pair = together(grad_w_gate, grad_out, grad_query, grad_pair)
    side = add_up(exchange_near(jnp.concatenate([grad_out, grad_query], axis=2), nz, own_z))
    grad_w_up = swap(after(grad_w_up, grad_w_gate), CTX).reshape(ctx, share, -1)
    grad_pair = add_up(exchange_near(over_y(over_x(grad_pair)), nz, own_z))
    grad_w_out, grad_w_query = side[:, :WIDTH], side[:, WIDTH:]
    grad_w_key, grad_w_value = grad_pair[:, :KV_WIDTH], grad_pair[:, KV_WIDTH:]
    output = middle + add_up(forth)
    grad_w_gate, grad_w_up = columns_in(grad_w_gate, grad_w_up, seq, ctx, run, padded)

    sums = sum_all(jnp.concatenate([norm_attn_sum, norm_mlp_sum, bias], axis=1), seq, nz)[0]
    number = place * ctx + index
    mine = lambda start, size: lax.dynamic_slice_in_dim(sums, start + number * size, size)
    g_norm_attn, g_norm_mlp, g_b_query = (mine(n * WIDTH, share) for n in range(3))
    g_b_key = sums[3 * WIDTH:3 * WIDTH + KV_WIDTH]
    g_b_value = mine(3 * WIDTH + KV_WIDTH, vshare)
    return (
        output,
        grad_tokens,
        grad_w_query,
        g_b_query,
        grad_w_key,
        g_b_key,
        grad_w_value,
        g_b_value,
        grad_w_out,
        g_norm_attn,
        grad_w_gate,
        grad_w_up,
        grad_w_down,
        g_norm_mlp,
    )


def solution(mesh):
    seq, ctx = mesh.shape["seq"], mesh.shape["ctx"]
    rows2, rows1 = P(ALL, None), P(ALL)
    return jax.shard_map(
        functools.partial(body, seq=seq, ctx=ctx),
        mesh=Mesh(mesh.devices.reshape(seq, ctx // 2, 2), ALL),
        in_specs=(
            rows2,
            P("seq", None),
            rows2,
            rows1,
            rows2,
            P(),
            rows2,
            rows1,
            rows2,
            rows1,
            rows2,
            rows2,
            rows2,
            rows1,
            rows2,
        ),
        out_specs=(
            rows2,
            rows2,
            rows2,
            rows1,
            rows2,
            P(),
            rows2,
            rows1,
            rows2,
            rows1,
            rows2,
            rows2,
            rows2,
            rows1,
        ),
        check_vma=False,
    )
```

```python
import functools
import math

import jax
import jax.numpy as jnp
from jax import lax
from jax.experimental import pallas as pl
from jax.experimental.pallas import tpu as pltpu
from jax.sharding import Mesh
from jax.sharding import PartitionSpec as P

HEADS = 12
KV_HEADS = 2
HEAD_DIM = 128
WIDTH = 1536
KV_WIDTH = 256
GROUP = HEADS // KV_HEADS
QKV = WIDTH + 2 * KV_WIDTH
LANES = 128

EPS = 1e-06
THETA = 1000000.0
NEGATIVE = -1e30
FACTOR = HEAD_DIM ** (-0.5)
VMEM_LIMIT = 58 * 1024 * 1024

CTX = ("z", "y")
ALL = ("seq", "z", "y")
BF = jnp.bfloat16
F32 = jnp.float32
LEFT = 1024
VMEM = pl.BlockSpec(memory_space=pltpu.VMEM)
SMEM = pl.BlockSpec(memory_space=pltpu.SMEM)


def shape(dims, kind):
    return jax.ShapeDtypeStruct(dims, kind)


def cost(flops, nbytes, exps=0):
    return pl.CostEstimate(flops=int(flops), bytes_accessed=int(nbytes), transcendentals=int(exps))


def whole(value):
    return pl.BlockSpec(value.shape, lambda i: (0,) * value.ndim)


def params():
    return pltpu.CompilerParams(vmem_limit_bytes=VMEM_LIMIT)


def inverse_rms(values):
    return lax.rsqrt(jnp.mean(values * values, axis=-1, keepdims=True) + EPS)


def matmul(left, right):
    return jnp.dot(left, right, preferred_element_type=F32)


def against(left, weight):
    return lax.dot_general(left, weight, (((1,), (1,)), ((), ())), preferred_element_type=F32)


def outer(left, right):
    return lax.dot_general(left, right, (((0,), (0,)), ((), ())), preferred_element_type=F32)


def rope_tables(positions):
    half = HEAD_DIM // 2
    freqs = THETA ** (-(2.0 * jnp.arange(half, dtype=F32)) / HEAD_DIM)
    angles = positions.astype(F32)[:, None] * freqs[None, :]
    cosine, sine = jnp.cos(angles), jnp.sin(angles)
    return jnp.concatenate([cosine, cosine], axis=-1), jnp.concatenate([-sine, sine], axis=-1)


def rotate(head, cosine, sine):
    return head * cosine + pltpu.roll(head, HEAD_DIM // 2, 1) * sine


def rotate_back(head, cosine, sine):
    return head * cosine - pltpu.roll(head, HEAD_DIM // 2, 1) * sine


def columns_out_kernel(gate_ref, up_ref, out_ref, *, seq, ctx, run, padded):
    chunk = seq * padded
    rows = gate_ref.shape[0]
    blank = jnp.zeros((rows, padded - run), BF)
    for which, ref in enumerate((gate_ref, up_ref)):
        for part in range(ctx):
            pieces = []
            for place in range(seq):
                start = (place * ctx + part) * run
                pieces += [ref[:, start:start + run], blank]
            out_ref[part, :, which * chunk:(which + 1) * chunk] = jnp.concatenate(pieces, axis=1)


def columns_out(gate, up, seq, ctx, run, padded):
    rows = gate.shape[0]
    return pl.pallas_call(
        functools.partial(columns_out_kernel, seq=seq, ctx=ctx, run=run, padded=padded),
        in_specs=[VMEM, VMEM],
        out_specs=VMEM,
        out_shape=shape((ctx, rows, 2 * seq * padded), BF),
        compiler_params=params(),
        cost_estimate=cost(0, 4 * gate.size * 2),
        name="columns_out",
    )(gate, up)


def columns_in_kernel(gate_in_ref, up_in_ref, gate_ref, up_ref, *, seq, ctx, run, padded):
    for in_ref, ref in ((gate_in_ref, gate_ref), (up_in_ref, up_ref)):
        pieces = []
        for place in range(seq):
            for part in range(ctx):
                pieces.append(in_ref[part, :, place * padded:place * padded + run])
        ref[...] = jnp.concatenate(pieces, axis=1).astype(F32)


def columns_in(gate, up, seq, ctx, run, padded):
    rows = gate.shape[1]
    return pl.pallas_call(
        functools.partial(columns_in_kernel, seq=seq, ctx=ctx, run=run, padded=padded),
        in_specs=[VMEM, VMEM],
        out_specs=[VMEM, VMEM],
        out_shape=[shape((rows, seq * ctx * run), F32)] * 2,
        compiler_params=params(),
        cost_estimate=cost(0, gate.size * 12),
        name="columns_in",
    )(gate, up)


def runs_of(core, own_ref, other_ref):
    run = own_ref.shape[0] // 2
    for x in range(2):
        for flip, ref in enumerate((own_ref, other_ref)):
            start = pl.multiple_of((2 * x + (core ^ flip)) * run, LANES)
            yield pl.ds(start, run), ref, slice(x * run, (x + 1) * run)


def times(core, left_ref, own_ref, other_ref, width):
    total = None
    for lanes, ref, rows in runs_of(core, own_ref, other_ref):
        term = matmul(left_ref[:, lanes], ref[rows, :width])
        total = term if total is None else total + term
    return total


def project_kernel(
    core_ref, tokens_ref, left_ref, left_other_ref, right_ref, right_other_ref,
    gain_ref, qbias_ref, kbias_ref, vbias_ref, cos_ref, sin_ref,
    normed_ref, query_ref, pair_out_ref,
):
    core = core_ref[0]
    inputs = tokens_ref[...].astype(F32)
    normed_ref[...] = (inputs * inverse_rms(inputs) * gain_ref[...]).astype(BF)
    left = times(core, normed_ref, left_ref, left_other_ref, LEFT)
    right = times(core, normed_ref, right_ref, right_other_ref, QKV - LEFT)
    query = jnp.concatenate([left, right[:, :WIDTH - LEFT]], axis=1) + qbias_ref[...]
    pair = right[:, WIDTH - LEFT:]
    key = pair[:, :KV_WIDTH] + kbias_ref[...]
    cosine, sine = cos_ref[...], sin_ref[...]
    for h in range(HEADS):
        lanes = slice(h * HEAD_DIM, (h + 1) * HEAD_DIM)
        query_ref[:, lanes] = rotate(query[:, lanes], cosine, sine).astype(BF)
    for g in range(KV_HEADS):
        lanes = slice(g * HEAD_DIM, (g + 1) * HEAD_DIM)
        turned = rotate(key[:, lanes], cosine, sine).astype(BF)
        for i in range(pair_out_ref.shape[0]):
            pair_out_ref[i, :, lanes] = turned
    value = (pair[:, KV_WIDTH:] + vbias_ref[...]).astype(BF)
    for i in range(pair_out_ref.shape[0]):
        pair_out_ref[i, :, KV_WIDTH:] = value


def project(core, tokens, left, right, gain, qbias, kbias, vbias, cosine, sine, copies):
    rows = tokens.shape[0]
    return pl.pallas_call(
        project_kernel,
        in_specs=[SMEM] + [VMEM] * 11,
        out_specs=[VMEM] * 3,
        out_shape=[shape((rows, WIDTH), BF), shape((rows, WIDTH), BF), shape((copies, rows, 2 * KV_WIDTH), BF)],
        compiler_params=params(),
        cost_estimate=cost(2 * rows * WIDTH * QKV, 2 * WIDTH * QKV + 6 * rows * WIDTH),
        name="project",
    )(core, tokens, *left, *right, gain, qbias, kbias, vbias, cosine, sine)


def vectors_kernel(core_ref, own_ref, other_ref, out_ref):
    for lanes, ref, rows in runs_of(core_ref[0], own_ref, other_ref):
        out_ref[:, lanes] = ref[rows, :].astype(F32).T[:out_ref.shape[0]]


def vectors_of(core, right, count):
    depth, width = right[0].shape
    block = pl.BlockSpec((depth, LANES), lambda i: (0, width // LANES - 1))
    return pl.pallas_call(
        vectors_kernel,
        grid=(1,),
        in_specs=[SMEM, block, block],
        out_specs=pl.BlockSpec((count, 2 * depth), lambda i: (0, 0)),
        out_shape=shape((count, 2 * depth), F32),
        compiler_params=params(),
        cost_estimate=cost(0, 4 * depth * LANES),
        name="vectors",
    )(core, *right)


def allowed_of(lo_ref, hi_ref, rows, length):
    places = lax.broadcasted_iota(jnp.int32, (rows, length), 1)
    return (places >= lo_ref[...]) & (places <= hi_ref[...])


def heads_per_step(length):
    return 3 if length <= 1024 else 1


def lanes_of(i):
    return slice(i * HEAD_DIM, (i + 1) * HEAD_DIM)


def forward_kernel(q_ref, k_ref, v_ref, lo_ref, hi_ref, mixed_ref, logsum_ref):
    keys, values = k_ref[...], v_ref[...]
    allowed = allowed_of(lo_ref, hi_ref, q_ref.shape[0], keys.shape[0])
    for i in range(logsum_ref.shape[0]):
        scores = jnp.where(allowed, against(q_ref[:, lanes_of(i)], keys) * FACTOR, NEGATIVE)
        top = jnp.max(scores, axis=-1, keepdims=True)
        weights = jnp.exp(scores - top)
        total = jnp.sum(weights, axis=-1, keepdims=True)
        shares = (weights * (1.0 / total)).astype(BF)
        mixed_ref[:, lanes_of(i)] = matmul(shares, values).astype(BF)
        logsum_ref[i] = top + jnp.log(total)


def attention_specs(rows, length, many):
    steps = GROUP // many
    head = pl.BlockSpec((rows, many * HEAD_DIM), lambda h: (0, h))
    key = pl.BlockSpec((length, HEAD_DIM), lambda h: (0, h // steps))
    value = pl.BlockSpec((length, HEAD_DIM), lambda h: (0, KV_HEADS + h // steps))
    column = pl.BlockSpec((rows, 1), lambda h: (0, 0))
    stat = pl.BlockSpec((many, rows, 1), lambda h: (h, 0, 0))
    return head, key, value, column, stat


def attention_forward(queries, pair, lo, hi):
    rows, length = queries.shape[0], pair.shape[0]
    many = heads_per_step(length)
    head, key, value, column, stat = attention_specs(rows, length, many)
    return pl.pallas_call(
        forward_kernel,
        grid=(HEADS // many,),
        in_specs=[head, key, value, column, column],
        out_specs=[head, stat],
        out_shape=[shape((rows, WIDTH), BF), shape((HEADS, rows, 1), F32)],
        compiler_params=params(),
        cost_estimate=cost(4 * rows * length * WIDTH, 4 * length * KV_WIDTH + 4 * rows * WIDTH, rows * length * HEADS),
        name="attention_forward",
    )(queries, pair, pair, lo, hi)


def backward_kernel(
    core_ref, q_ref, k_ref, v_ref, g_ref, lo_ref, hi_ref, logsum_ref, cos_ref, sin_ref, cosq_ref, sinq_ref,
    normed_ref, mixed_ref, branch_ref, dq_ref, dkv_ref, keep_ref, send_ref, dk_sum, dv_sum, turned_ref,
):
    step = pl.program_id(0)
    many = logsum_ref.shape[0]
    group = step // (GROUP // many)
    member = lax.rem(step, GROUP // many)

    @pl.when(step == 0)
    def _():
        turned_ref[...] = normed_ref[...].astype(F32).T.astype(BF)

    keys, values = k_ref[...], v_ref[...]
    allowed = allowed_of(lo_ref, hi_ref, q_ref.shape[0], keys.shape[0])
    dk, dv = None, None
    for i in range(many):
        queries, grads = q_ref[:, lanes_of(i)], g_ref[:, lanes_of(i)]
        scores = jnp.where(allowed, against(queries, keys) * FACTOR, NEGATIVE)
        shares = jnp.where(allowed, jnp.exp(scores - logsum_ref[i]), 0.0)
        grad_shares = against(grads, values)
        delta = jnp.sum(shares * grad_shares, axis=-1, keepdims=True)
        grad_scores = (shares * (grad_shares - delta)).astype(BF)
        dq = matmul(grad_scores, keys) * FACTOR
        dq_ref[:, lanes_of(i)] = rotate_back(dq, cosq_ref[...], sinq_ref[...]).astype(BF)
        dk_here = outer(grad_scores, queries) * FACTOR
        dv_here = outer(shares.astype(BF), grads)
        dk, dv = (dk_here, dv_here) if i == 0 else (dk + dk_here, dv + dv_here)

    @pl.when(member == 0)
    def _():
        dk_sum[...] = dk
        dv_sum[...] = dv

    @pl.when(member > 0)
    def _():
        dk_sum[...] += dk
        dv_sum[...] += dv

    @pl.when(member == GROUP // many - 1)
    def _():
        here = pl.multiple_of(group * HEAD_DIM, HEAD_DIM)
        there = pl.multiple_of(KV_WIDTH + group * HEAD_DIM, HEAD_DIM)
        dkv_ref[:, pl.ds(here, HEAD_DIM)] = rotate_back(dk_sum[...], cos_ref[...], sin_ref[...]).astype(BF)
        dkv_ref[:, pl.ds(there, HEAD_DIM)] = dv_sum[...].astype(BF)

    core = core_ref[0]
    width = many * HEAD_DIM
    columns = pl.ds(pl.multiple_of(step * width, HEAD_DIM), width)
    for lanes, ref, rows in runs_of(core, keep_ref, send_ref):
        ref[rows, columns] = matmul(turned_ref[lanes, :], dq_ref[...]).astype(BF)
    run = keep_ref.shape[0] // 2
    steps = run // width
    place = step // steps
    row = pl.multiple_of(place // 2 * run + lax.rem(step, steps) * width, HEAD_DIM)
    terms = outer(mixed_ref[...], branch_ref[...]).astype(BF)
    mine = lax.rem(place, 2) == core

    @pl.when(mine)
    def _():
        keep_ref[pl.ds(row, width), WIDTH:] = terms

    @pl.when(jnp.logical_not(mine))
    def _():
        send_ref[pl.ds(row, width), WIDTH:] = terms


def attention_backward(
    core, queries, pair, grads, lo, hi, logsum, cosine, sine, cosine_own, sine_own, normed, mixed, grad_branch
):
    rows, length = queries.shape[0], pair.shape[0]
    once = pl.Buffered(1)
    many = heads_per_step(length)
    head, key, value, column, stat = attention_specs(rows, length, many)
    fixed = lambda x: pl.BlockSpec(x.shape, lambda h: (0, 0), pipeline_mode=once)
    terms = shape((WIDTH // 2, 2 * WIDTH), BF)
    return pl.pallas_call(
        backward_kernel,
        grid=(HEADS // many,),
        in_specs=[SMEM, head, key, value, head, column, column, stat]
        + [fixed(x) for x in (cosine, sine, cosine_own, sine_own, normed)]
        + [head, fixed(grad_branch)],
        out_specs=[head, pl.BlockSpec((length, 2 * KV_WIDTH), lambda h: (0, 0))]
        + [pl.BlockSpec(terms.shape, lambda h: (0, 0))] * 2,
        out_shape=[shape((rows, WIDTH), BF), shape((length, 2 * KV_WIDTH), BF), terms, terms],
        scratch_shapes=[
            pltpu.VMEM((length, HEAD_DIM), F32),
            pltpu.VMEM((length, HEAD_DIM), F32),
            pltpu.VMEM((WIDTH, rows), BF),
        ],
        compiler_params=params(),
        cost_estimate=cost(10 * rows * length * WIDTH, 16 * length * KV_WIDTH, rows * length * HEADS),
        name="attention_backward",
    )(core, queries, pair, pair, grads, lo, hi, logsum, cosine, sine, cosine_own, sine_own, normed, mixed, grad_branch)


def branch_kernel(core_ref, mixed_ref, *refs):
    weights, (tokens_ref, gain_ref, middle_ref, first_ref, second_ref) = refs[:4], refs[4:]
    width = weights[0].shape[1]
    parts = [times(core_ref[0], mixed_ref, weights[2 * i], weights[2 * i + 1], width) for i in range(2)]
    middle = tokens_ref[...].astype(F32) + jnp.concatenate(parts, axis=1)
    middle_ref[...] = middle
    normed = (middle * inverse_rms(middle) * gain_ref[...]).astype(BF)
    half = first_ref.shape[1]
    for i in range(first_ref.shape[0]):
        first_ref[i] = normed[:half]
        second_ref[i] = normed[half:]


def branch(core, mixed, out_weight, tokens, gain, copies):
    rows = mixed.shape[0]
    return pl.pallas_call(
        branch_kernel,
        in_specs=[SMEM] + [VMEM] * 7,
        out_specs=[VMEM] * 3,
        out_shape=[shape((rows, WIDTH), F32)] + [shape((copies, rows // 2, WIDTH), BF)] * 2,
        compiler_params=params(),
        cost_estimate=cost(2 * rows * WIDTH * WIDTH, 2 * WIDTH * WIDTH),
        name="branch",
    )(core, mixed, *out_weight, tokens, gain)


def mlp_kernel(
    near_ref, other_ref, cot_near_ref, cot_other_ref, gate_ref, up_ref, down_ref,
    hidden_ref, grad_gate_ref, grad_up_ref, back_near_ref, back_other_ref, forth_near_ref, forth_other_ref,
):
    rows = near_ref.shape[0]
    tokens = jnp.concatenate([near_ref[...], other_ref[...]], axis=0)
    cotangent = jnp.concatenate([cot_near_ref[...], cot_other_ref[...]], axis=0)
    gate = matmul(tokens, gate_ref[...])
    upper = matmul(tokens, up_ref[...])
    grad_hidden = against(cotangent, down_ref[...])
    logistic = 1.0 / (1.0 + jnp.exp(-gate))
    silu = gate * logistic
    hidden = (silu * upper).astype(BF)
    hidden_ref[...] = hidden
    grad_gate = (grad_hidden * upper * logistic * (1.0 + gate * (1.0 - logistic))).astype(BF)
    grad_upper = (grad_hidden * silu).astype(BF)
    grad_gate_ref[...] = grad_gate
    grad_up_ref[...] = grad_upper
    back = (against(grad_gate, gate_ref[...]) + against(grad_upper, up_ref[...])).astype(BF)
    back_near_ref[...] = back[:rows]
    back_other_ref[...] = back[rows:]
    forth = matmul(hidden, down_ref[...]).astype(BF)
    forth_near_ref[...] = forth[:rows]
    forth_other_ref[...] = forth[rows:]


def mlp(near, other, cot_near, cot_other, gate_up, down):
    rows = 2 * near.shape[0]
    chunk = down.shape[0]
    part = lambda n: pl.BlockSpec((WIDTH, chunk), lambda i: (0, n))
    made = [shape((rows, chunk), BF)] * 3 + [shape(near.shape, BF)] * 4
    return pl.pallas_call(
        mlp_kernel,
        grid=(1,),
        in_specs=[whole(near)] * 4 + [part(0), part(1), whole(down)],
        out_specs=[whole(x) for x in made],
        out_shape=made,
        compiler_params=params(),
        cost_estimate=cost(12 * rows * WIDTH * chunk, 6 * WIDTH * chunk + 14 * rows * WIDTH, rows * chunk),
        name="mlp",
    )(near, other, cot_near, cot_other, gate_up, gate_up, down)


def outer_kernel(*refs, counts):
    blocks, position = [], 0
    for count in counts:
        blocks.append(jnp.concatenate([ref[...] for ref in refs[position:position + count]], axis=0))
        position += count
    for right, out_ref in zip(blocks[1:], refs[position:]):
        out_ref[...] = outer(blocks[0], right).astype(BF)


def outer_blocks(lefts, rights, name):
    depth = sum(x.shape[0] for x in lefts)
    width = lefts[0].shape[1]
    across = [blocks[0].shape[1] for blocks in rights]
    tile = 384 if width % 384 == 0 else width
    flat = [x for blocks in rights for x in blocks]
    return pl.pallas_call(
        functools.partial(outer_kernel, counts=(len(lefts), *map(len, rights))),
        grid=(width // tile,),
        in_specs=[pl.BlockSpec((x.shape[0], tile), lambda i: (0, i)) for x in lefts]
        + [pl.BlockSpec(x.shape, lambda i: (0, 0), pipeline_mode=pl.Buffered(1)) for x in flat],
        out_specs=[pl.BlockSpec((tile, n), lambda i: (i, 0)) for n in across],
        out_shape=[shape((width, n), BF) for n in across],
        compiler_params=params(),
        cost_estimate=cost(2 * depth * width * sum(across), 2 * (depth + width) * (width + sum(across))),
        name=name,
    )(*lefts, *flat)


def middle_kernel(
    core_ref, first_ref, middle_ref, cotangent_ref, gain_ref, *refs
):
    weights, second, (grad_ref, branch_ref, mixed_ref, norm_ref) = refs[:4], refs[4:-4], refs[-4:]
    total = jnp.concatenate(
        [jnp.sum(first_ref[...].astype(F32), axis=0), sum(ref[...].astype(F32) for ref in second)], axis=0
    )
    middle = middle_ref[...]
    scale = inverse_rms(middle)
    norm_ref[...] = jnp.sum(total * middle * scale, axis=0, keepdims=True)
    weighted = total * gain_ref[...]
    grad = (
        cotangent_ref[...].astype(F32)
        + scale * weighted
        - middle * (scale * scale * scale) * jnp.mean(weighted * middle, axis=-1, keepdims=True)
    )
    grad_ref[...] = grad
    low = grad.astype(BF)
    branch_ref[...] = low
    width = weights[0].shape[1]
    core = core_ref[0]
    for first, second in zip(runs_of(core, *weights[:2]), runs_of(core, *weights[2:])):
        lanes, ref, rows = first
        mixed_ref[:, lanes] = (
            against(low[:, :width], ref[rows, :]) + against(low[:, width:], second[1][rows, :])
        ).astype(BF)


def middle_back(core, terms, middle, cotangent, gain, out_weight):
    rows = middle.shape[0]
    return pl.pallas_call(
        middle_kernel,
        in_specs=[SMEM] + [VMEM] * (8 + len(terms[1])),
        out_specs=[VMEM] * 4,
        out_shape=[shape((rows, WIDTH), F32), shape((rows, WIDTH), BF), shape((rows, WIDTH), BF), shape((1, WIDTH), F32)],
        compiler_params=params(),
        cost_estimate=cost(2 * rows * WIDTH * WIDTH, 2 * WIDTH * WIDTH + 20 * rows * WIDTH),
        name="middle_back",
    )(core, terms[0], middle, cotangent, gain, *out_weight, *terms[1])


def tokens_kernel(
    core_ref, grads_ref, left_ref, left_other_ref, right_ref, right_other_ref, tokens_ref, gain_ref, middle_ref,
    out_ref, norm_ref, bias_ref, total_ref,
):
    grads = grads_ref[...]
    bias_ref[...] = jnp.sum(grads.astype(F32), axis=0, keepdims=True)
    core = core_ref[0]
    for first, second in zip(runs_of(core, left_ref, left_other_ref), runs_of(core, right_ref, right_other_ref)):
        lanes, ref, rows = first
        total_ref[:, lanes] = against(grads[:, :LEFT], ref[rows, :]) + against(
            grads[:, LEFT:], second[1][rows, :QKV - LEFT]
        )
    grad_normed = total_ref[...]
    inputs = tokens_ref[...].astype(F32)
    scale = inverse_rms(inputs)
    norm_ref[...] = jnp.sum(grad_normed * inputs * scale, axis=0, keepdims=True)
    weighted = grad_normed * gain_ref[...]
    out_ref[...] = (
        middle_ref[...]
        + scale * weighted
        - inputs * (scale * scale * scale) * jnp.mean(weighted * inputs, axis=-1, keepdims=True)
    )


def tokens_back(core, grads, left, right, tokens, gain, middle):
    rows = tokens.shape[0]
    return pl.pallas_call(
        tokens_kernel,
        in_specs=[SMEM] + [VMEM] * 8,
        out_specs=[VMEM] * 3,
        out_shape=[shape((rows, WIDTH), F32), shape((1, WIDTH), F32), shape((1, QKV), F32)],
        scratch_shapes=[pltpu.VMEM((rows, WIDTH), F32)],
        compiler_params=params(),
        cost_estimate=cost(2 * rows * WIDTH * QKV, 2 * WIDTH * QKV + 12 * rows * WIDTH),
        name="tokens_back",
    )(core, grads, *left, *right, tokens, gain, middle)


def gather(value, axis):
    return lax.all_gather(value, axis, axis=0, tiled=True)


def scatter_sum(value, axis):
    return lax.psum_scatter(value, axis, scatter_dimension=0, tiled=True)


def swap(value, axis):
    return lax.all_to_all(value, axis, 0, 0, tiled=True)


def hop(value, axis, size=2, flip=1):
    return lax.ppermute(value, axis, [(i, i ^ flip) for i in range(size)])


def after(value, *earlier):
    return lax.optimization_barrier((value, *earlier))[0]


def together(*values):
    return lax.optimization_barrier(values)


def gather_near(value, nz):
    copies = jnp.broadcast_to(value[None], (nz, *value.shape)).reshape(-1, value.shape[1])
    return swap(copies, "z").reshape(nz, *value.shape)


def share_near(copies):
    return swap(copies.reshape(-1, copies.shape[2]), "z").reshape(copies.shape)


def add_low(left, right):
    return (left.astype(F32) + right.astype(F32)).astype(BF)


def exchange_near(blocks, nz, own_z):
    out = [lax.dynamic_index_in_dim(blocks, own_z, 0, keepdims=False)]
    for flip in range(1, nz):
        out.append(hop(lax.dynamic_index_in_dim(blocks, own_z ^ flip, 0, keepdims=False), "z", nz, flip))
    return out


def add_up(blocks):
    total = blocks[0].astype(F32)
    for block in blocks[1:]:
        total = total + block.astype(F32)
    return total


def pair(own, other, bit, axis):
    first, second = jnp.where(bit == 0, own, other), jnp.where(bit == 0, other, own)
    return jnp.stack([first, second], axis=axis)


def gather_z(value, nz, own_z):
    blocks = jnp.stack([value] + [hop(value, "z", nz, j) for j in range(1, nz)])
    return jnp.concatenate([lax.dynamic_slice_in_dim(blocks, own_z ^ j, 1) for j in range(nz)], axis=0)


def halve(value, axis, flip, size, bit, dim):
    keep = lax.dynamic_index_in_dim(value, bit, dim, keepdims=False)
    send = lax.dynamic_index_in_dim(value, 1 - bit, dim, keepdims=False)
    return add_low(keep, hop(send, axis, size, flip))


def sum_all(value, seq, nz):
    for axis, size in (("seq", seq), ("y", 2), ("z", nz)):
        flip = 1
        while flip < size:
            value = value + hop(value, axis, size, flip)
            flip *= 2
    return value


def body(
    tokens,
    segments,
    w_query,
    b_query,
    w_key,
    b_key,
    w_value,
    b_value,
    w_out,
    norm_attn,
    w_gate,
    w_up,
    w_down,
    norm_mlp,
    cotangent,
    *,
    seq,
    ctx,
):
    rows = tokens.shape[0]
    half = rows // 2
    nz = ctx // 2
    devices = seq * ctx
    share = w_query.shape[0]
    vshare = b_value.shape[0]
    run = w_down.shape[0]
    unit = LANES // math.gcd(LANES, seq)
    padded = -(-run // unit) * unit
    ident = segments[0]
    length = ident.shape[0]
    own_z, own_y, place = lax.axis_index("z"), lax.axis_index("y"), lax.axis_index("seq")
    index = 2 * own_z + own_y

    small = jnp.stack([norm_attn, norm_mlp, b_query, jnp.pad(b_value, (0, share - vshare))], axis=1)
    small = jnp.pad(small, ((0, 0), (0, LANES - 4)))
    projections = jnp.concatenate([w_query, w_key, w_value, small], axis=1)
    x, core = place // 2, place % 2
    over = lambda v, axis: hop(v, "seq", seq, 2) if axis == "x" else hop(v, "seq", seq, 1) if axis == "core" else hop(v, "y")
    flat = lambda v: v.reshape(2 * ctx * share, v.shape[-1])
    cuts = [slice(i * half, (i + 1) * half) for i in range(2)]
    count = nz * half
    cosine, sine = rope_tables(jnp.arange(length, dtype=jnp.int32) - ident)
    offset = index * rows
    hi = (offset + jnp.arange(rows, dtype=jnp.int32))[:, None]
    lo = lax.dynamic_slice_in_dim(ident, offset, rows)[:, None]
    tables = [cosine, sine] + [lax.dynamic_slice_in_dim(x, offset, rows) for x in (cosine, sine)] + [lo, hi]
    turned = columns_out(w_gate, w_up, seq, ctx, run, padded).reshape(ctx * share, -1)
    near = gather_near(after(projections, turned), nz)
    turned = swap(after(turned, near), CTX)
    left, right = near[:, :, :LEFT], near[:, :, LEFT:]
    left_got, right_got, near, tables = together(
        over(left, "y"), over(right, "x"), gather_z(after(w_out, near), nz, own_z), tables
    )
    left, right = pair(left, left_got, own_y, 1), pair(right, right_got, x, 0)
    out_left, out_right = near[:, :, :WIDTH // 2], near[:, :, WIDTH // 2:]
    left_got, right_got, out_left_got, out_right_got = together(
        over(left, "x"), over(right, "y"), over(out_left, "y"), over(out_right, "x")
    )
    left, right = flat(pair(left, left_got, x, 0)), flat(pair(right, right_got, own_y, 2))
    out_left, out_right = pair(out_left, out_left_got, own_y, 1), pair(out_right, out_right_got, x, 0)
    left_got, right_got, out_left_got, out_right_got = together(
        over(left, "core"), over(right, "core"), over(out_left, "x"), over(out_right, "y")
    )
    left, right = (left, left_got), (right, right_got)
    out_left, out_right = flat(pair(out_left, out_left_got, x, 0)), flat(pair(out_right, out_right_got, own_y, 2))
    out_weight = (out_left, over(out_left, "core"), out_right, over(out_right, "core"))
    down = jnp.pad(w_down, ((0, padded - run), (0, 0)))
    down = gather(down, "seq")
    gate_up = gather(after(turned, left_got), "seq")
    cotangent_low = after(cotangent, turned)
    cot_near = [gather_near(cotangent_low[cuts[0]], nz).reshape(count, WIDTH)]
    cosine, sine, cosine_own, sine_own, lo, hi = tables
    core = core.astype(jnp.int32)[None]
    vectors = vectors_of(core, right, 8)
    attn_gain, mlp_gain, query_bias = vectors[0:1], vectors[1:2], vectors[2:3]
    value_bias = vectors[3].reshape(devices, share)[:, :vshare].reshape(1, KV_WIDTH)

    normed, queries, kv = project(
        core, tokens, left, right, attn_gain, query_bias, b_key.astype(F32)[None], value_bias, cosine_own, sine_own, nz
    )
    near = share_near(after(kv, cot_near[0]))
    cot_near.append(gather_near(after(cotangent, near)[cuts[1]], nz).reshape(count, WIDTH))
    other = hop(near, "y")
    cot_other = [hop(after(x, other), "y") for x in cot_near]
    kv = pair(near, other, own_y, 1).reshape(length, 2 * KV_WIDTH)
    mixed, logsum = attention_forward(queries, kv, lo, hi)
    mixed, out_weight, cot_other[0] = together(mixed, out_weight, cot_other[0])
    middle, *copies = branch(core, mixed, out_weight, tokens, mlp_gain, nz)

    copies[1] = after(copies[1], cot_near[1], cot_other[1])
    x_near = [share_near(x).reshape(count, WIDTH) for x in copies]
    x_other = [hop(x, "y") for x in x_near]
    runs = [mlp(x_near[0], x_other[0], cot_near[0], cot_other[0], gate_up, down)]
    x_other[1] = after(x_other[1], *runs[0])
    runs.append(mlp(x_near[1], x_other[1], cot_near[1], cot_other[1], gate_up, down))
    hidden, grads_gate, grads_up, back_near, back_other, forth_near, forth_other = zip(*runs)
    sums = []
    for i in range(2):
        sums.append(add_low(back_near[i], hop(after(back_other[i], *sums), "y")))
    far = [swap(sums[0], "z").reshape(nz, half, WIDTH), exchange_near(sums[1].reshape(nz, half, WIDTH), nz, own_z)]
    x_all = [x_near[0], x_other[0], x_near[1], x_other[1]]
    cots = [cot_near[0], cot_other[0], cot_near[1], cot_other[1]]
    forth_got = [hop(after(x, *sums), "y") for x in forth_other]
    grads_gate, grads_up = after((grads_gate, grads_up), far, forth_got[0])
    grad_w_gate, grad_w_up = outer_blocks(x_all, [grads_gate, grads_up], "gate_up_grads")
    grad_w_gate, grad_w_up = scatter_sum(grad_w_gate, "seq"), scatter_sum(grad_w_up, "seq")

    grad_middle, grad_branch, grad_mixed, norm_mlp_sum = middle_back(core, far, middle, cotangent, mlp_gain, out_weight)
    grad_mixed, forth_got = together(grad_mixed, forth_got)
    dq, dkv, keep, send = attention_backward(
        core, queries, kv, grad_mixed, lo, hi, logsum, cosine, sine, cosine_own, sine_own, normed, mixed, grad_branch
    )
    forth = jnp.concatenate(
        [add_low(x, y).reshape(nz, half, WIDTH) for x, y in zip(forth_near, forth_got)], axis=1
    )
    forth = exchange_near(forth, nz, own_z)
    terms = swap(dkv, CTX).reshape(ctx, rows, 2 * KV_WIDTH)
    terms = jnp.sum(terms.astype(F32), axis=0).astype(BF)

    over_core = lambda v: halve(v, "seq", 1, seq, place % 2, 1)
    over_x = lambda v: halve(v, "seq", 2, seq, place // 2, 0)
    over_y = lambda v: halve(v, "y", 1, 2, own_y, v.ndim - 3)
    sides = add_low(keep, over(send, "core")).reshape(2, nz, 2, share, -1)
    grad_query, grad_out = over_x(sides[..., :WIDTH]), over_y(sides[..., WIDTH:])
    (grad_w_down,) = outer_blocks(after(hidden, sides), [cots], "down_grads")
    grad_w_down = scatter_sum(grad_w_down, "seq")[:run].astype(F32)
    grad_w_gate = swap(after(grad_w_gate, terms), CTX).reshape(ctx, share, -1)
    (grad_pair,) = outer_blocks([normed], [[after(terms, grad_out, grad_query)]], "pair_grads")
    grad_tokens, norm_attn_sum, bias = tokens_back(
        core, jnp.concatenate([dq, after(terms, grad_pair)], axis=1), left, right, tokens, attn_gain, grad_middle
    )
    grad_pair, bias, forth, grad_w_gate = together(grad_pair, bias, forth, grad_w_gate)
    grad_w_up = swap(after(grad_w_up, grad_w_gate), CTX).reshape(ctx, share, -1)
    grad_pair = over_core(grad_pair.reshape(2, 2, nz, 2, share, -1))
    grad_out, grad_query = over_x(grad_out), over_y(grad_query)
    grad_w_up, grad_out, grad_query, grad_pair = together(grad_w_up, grad_out, grad_query, grad_pair)
    side = add_up(exchange_near(jnp.concatenate([grad_out, grad_query], axis=2), nz, own_z))
    grad_pair = add_up(exchange_near(over_y(over_x(grad_pair)), nz, own_z))
    grad_w_out, grad_w_query = side[:, :WIDTH], side[:, WIDTH:]
    grad_w_key, grad_w_value = grad_pair[:, :KV_WIDTH], grad_pair[:, KV_WIDTH:]
    output = middle + add_up(forth)
    grad_w_gate, grad_w_up = columns_in(grad_w_gate, grad_w_up, seq, ctx, run, padded)

    sums = sum_all(jnp.concatenate([norm_attn_sum, norm_mlp_sum, bias], axis=1), seq, nz)[0]
    number = place * ctx + index
    mine = lambda start, size: lax.dynamic_slice_in_dim(sums, start + number * size, size)
    g_norm_attn, g_norm_mlp, g_b_query = (mine(n * WIDTH, share) for n in range(3))
    g_b_key = sums[3 * WIDTH:3 * WIDTH + KV_WIDTH]
    g_b_value = mine(3 * WIDTH + KV_WIDTH, vshare)
    return (
        output,
        grad_tokens,
        grad_w_query,
        g_b_query,
        grad_w_key,
        g_b_key,
        grad_w_value,
        g_b_value,
        grad_w_out,
        g_norm_attn,
        grad_w_gate,
        grad_w_up,
        grad_w_down,
        g_norm_mlp,
    )


def solution(mesh):
    seq, ctx = mesh.shape["seq"], mesh.shape["ctx"]
    rows2, rows1 = P(ALL, None), P(ALL)
    return jax.shard_map(
        functools.partial(body, seq=seq, ctx=ctx),
        mesh=Mesh(mesh.devices.reshape(seq, ctx // 2, 2), ALL),
        in_specs=(
            rows2,
            P("seq", None),
            rows2,
            rows1,
            rows2,
            P(),
            rows2,
            rows1,
            rows2,
            rows1,
            rows2,
            rows2,
            rows2,
            rows1,
            rows2,
        ),
        out_specs=(
            rows2,
            rows2,
            rows2,
            rows1,
            rows2,
            P(),
            rows2,
            rows1,
            rows2,
            rows1,
            rows2,
            rows2,
            rows2,
            rows1,
        ),
        check_vma=False,
    )
```

```python
import functools
import math

import jax
import jax.numpy as jnp
from jax import lax
from jax.experimental import pallas as pl
from jax.experimental.pallas import tpu as pltpu
from jax.sharding import Mesh
from jax.sharding import PartitionSpec as P

HEADS = 12
KV_HEADS = 2
HEAD_DIM = 128
WIDTH = 1536
KV_WIDTH = 256
GROUP = HEADS // KV_HEADS
QKV = WIDTH + 2 * KV_WIDTH
LANES = 128

EPS = 1e-06
THETA = 1000000.0
NEGATIVE = -1e30
FACTOR = HEAD_DIM ** (-0.5)
VMEM_LIMIT = 58 * 1024 * 1024

CTX = ("z", "y")
ALL = ("seq", "z", "y")
BF = jnp.bfloat16
F32 = jnp.float32
LEFT = 1024
VMEM = pl.BlockSpec(memory_space=pltpu.VMEM)
SMEM = pl.BlockSpec(memory_space=pltpu.SMEM)


def shape(dims, kind):
    return jax.ShapeDtypeStruct(dims, kind)


def cost(flops, nbytes, exps=0):
    return pl.CostEstimate(flops=int(flops), bytes_accessed=int(nbytes), transcendentals=int(exps))


def whole(value):
    return pl.BlockSpec(value.shape, lambda i: (0,) * value.ndim)


def params():
    return pltpu.CompilerParams(vmem_limit_bytes=VMEM_LIMIT)


def inverse_rms(values):
    return lax.rsqrt(jnp.mean(values * values, axis=-1, keepdims=True) + EPS)


def matmul(left, right):
    return jnp.dot(left, right, preferred_element_type=F32)


def against(left, weight):
    return lax.dot_general(left, weight, (((1,), (1,)), ((), ())), preferred_element_type=F32)


def outer(left, right):
    return lax.dot_general(left, right, (((0,), (0,)), ((), ())), preferred_element_type=F32)


def rope_tables(positions):
    half = HEAD_DIM // 2
    freqs = THETA ** (-(2.0 * jnp.arange(half, dtype=F32)) / HEAD_DIM)
    angles = positions.astype(F32)[:, None] * freqs[None, :]
    cosine, sine = jnp.cos(angles), jnp.sin(angles)
    return jnp.concatenate([cosine, cosine], axis=-1), jnp.concatenate([-sine, sine], axis=-1)


def rotate(head, cosine, sine):
    return head * cosine + pltpu.roll(head, HEAD_DIM // 2, 1) * sine


def rotate_back(head, cosine, sine):
    return head * cosine - pltpu.roll(head, HEAD_DIM // 2, 1) * sine


def columns_out_kernel(gate_ref, up_ref, out_ref, *, seq, ctx, run, padded):
    chunk = seq * padded
    rows = gate_ref.shape[0]
    blank = jnp.zeros((rows, padded - run), BF)
    for which, ref in enumerate((gate_ref, up_ref)):
        for part in range(ctx):
            pieces = []
            for place in range(seq):
                start = (place * ctx + part) * run
                pieces += [ref[:, start:start + run], blank]
            out_ref[part, :, which * chunk:(which + 1) * chunk] = jnp.concatenate(pieces, axis=1)


def columns_out(gate, up, seq, ctx, run, padded):
    rows = gate.shape[0]
    return pl.pallas_call(
        functools.partial(columns_out_kernel, seq=seq, ctx=ctx, run=run, padded=padded),
        in_specs=[VMEM, VMEM],
        out_specs=VMEM,
        out_shape=shape((ctx, rows, 2 * seq * padded), BF),
        compiler_params=params(),
        cost_estimate=cost(0, 4 * gate.size * 2),
        name="columns_out",
    )(gate, up)


def columns_in_kernel(gate_in_ref, up_in_ref, gate_ref, up_ref, *, seq, ctx, run, padded):
    for in_ref, ref in ((gate_in_ref, gate_ref), (up_in_ref, up_ref)):
        pieces = []
        for place in range(seq):
            for part in range(ctx):
                pieces.append(in_ref[part, :, place * padded:place * padded + run])
        ref[...] = jnp.concatenate(pieces, axis=1).astype(F32)


def columns_in(gate, up, seq, ctx, run, padded):
    rows = gate.shape[1]
    return pl.pallas_call(
        functools.partial(columns_in_kernel, seq=seq, ctx=ctx, run=run, padded=padded),
        in_specs=[VMEM, VMEM],
        out_specs=[VMEM, VMEM],
        out_shape=[shape((rows, seq * ctx * run), F32)] * 2,
        compiler_params=params(),
        cost_estimate=cost(0, gate.size * 12),
        name="columns_in",
    )(gate, up)


def runs_of(core, own_ref, other_ref):
    run = own_ref.shape[0] // 2
    for x in range(2):
        for flip, ref in enumerate((own_ref, other_ref)):
            start = pl.multiple_of((2 * x + (core ^ flip)) * run, LANES)
            yield pl.ds(start, run), ref, slice(x * run, (x + 1) * run)


def times(core, left_ref, own_ref, other_ref, width):
    total = None
    for lanes, ref, rows in runs_of(core, own_ref, other_ref):
        term = matmul(left_ref[:, lanes], ref[rows, :width])
        total = term if total is None else total + term
    return total


def project_kernel(
    core_ref, tokens_ref, left_ref, left_other_ref, right_ref, right_other_ref,
    gain_ref, qbias_ref, kbias_ref, vbias_ref, cos_ref, sin_ref,
    normed_ref, query_ref, pair_out_ref,
):
    core = core_ref[0]
    inputs = tokens_ref[...].astype(F32)
    normed_ref[...] = (inputs * inverse_rms(inputs) * gain_ref[...]).astype(BF)
    left = times(core, normed_ref, left_ref, left_other_ref, LEFT)
    right = times(core, normed_ref, right_ref, right_other_ref, QKV - LEFT)
    query = jnp.concatenate([left, right[:, :WIDTH - LEFT]], axis=1) + qbias_ref[...]
    pair = right[:, WIDTH - LEFT:]
    key = pair[:, :KV_WIDTH] + kbias_ref[...]
    cosine, sine = cos_ref[...], sin_ref[...]
    for h in range(HEADS):
        lanes = slice(h * HEAD_DIM, (h + 1) * HEAD_DIM)
        query_ref[:, lanes] = rotate(query[:, lanes], cosine, sine).astype(BF)
    for g in range(KV_HEADS):
        lanes = slice(g * HEAD_DIM, (g + 1) * HEAD_DIM)
        turned = rotate(key[:, lanes], cosine, sine).astype(BF)
        for i in range(pair_out_ref.shape[0]):
            pair_out_ref[i, :, lanes] = turned
    value = (pair[:, KV_WIDTH:] + vbias_ref[...]).astype(BF)
    for i in range(pair_out_ref.shape[0]):
        pair_out_ref[i, :, KV_WIDTH:] = value


def project(core, tokens, left, right, gain, qbias, kbias, vbias, cosine, sine, copies):
    rows = tokens.shape[0]
    return pl.pallas_call(
        project_kernel,
        in_specs=[SMEM] + [VMEM] * 11,
        out_specs=[VMEM] * 3,
        out_shape=[shape((rows, WIDTH), BF), shape((rows, WIDTH), BF), shape((copies, rows, 2 * KV_WIDTH), BF)],
        compiler_params=params(),
        cost_estimate=cost(2 * rows * WIDTH * QKV, 2 * WIDTH * QKV + 6 * rows * WIDTH),
        name="project",
    )(core, tokens, *left, *right, gain, qbias, kbias, vbias, cosine, sine)


def vectors_kernel(core_ref, own_ref, other_ref, out_ref):
    for lanes, ref, rows in runs_of(core_ref[0], own_ref, other_ref):
        out_ref[:, lanes] = ref[rows, :].astype(F32).T[:out_ref.shape[0]]


def vectors_of(core, right, count):
    depth, width = right[0].shape
    block = pl.BlockSpec((depth, LANES), lambda i: (0, width // LANES - 1))
    return pl.pallas_call(
        vectors_kernel,
        grid=(1,),
        in_specs=[SMEM, block, block],
        out_specs=pl.BlockSpec((count, 2 * depth), lambda i: (0, 0)),
        out_shape=shape((count, 2 * depth), F32),
        compiler_params=params(),
        cost_estimate=cost(0, 4 * depth * LANES),
        name="vectors",
    )(core, *right)


def allowed_of(lo_ref, hi_ref, rows, length):
    places = lax.broadcasted_iota(jnp.int32, (rows, length), 1)
    return (places >= lo_ref[...]) & (places <= hi_ref[...])


def heads_per_step(length):
    return 3 if length <= 1024 else 1


def lanes_of(i):
    return slice(i * HEAD_DIM, (i + 1) * HEAD_DIM)


def forward_kernel(q_ref, k_ref, v_ref, lo_ref, hi_ref, mixed_ref, logsum_ref):
    keys, values = k_ref[...], v_ref[...]
    allowed = allowed_of(lo_ref, hi_ref, q_ref.shape[0], keys.shape[0])
    for i in range(logsum_ref.shape[0]):
        scores = jnp.where(allowed, against(q_ref[:, lanes_of(i)], keys) * FACTOR, NEGATIVE)
        top = jnp.max(scores, axis=-1, keepdims=True)
        weights = jnp.exp(scores - top)
        total = jnp.sum(weights, axis=-1, keepdims=True)
        shares = (weights * (1.0 / total)).astype(BF)
        mixed_ref[:, lanes_of(i)] = matmul(shares, values).astype(BF)
        logsum_ref[i] = top + jnp.log(total)


def attention_specs(rows, length, many):
    steps = GROUP // many
    head = pl.BlockSpec((rows, many * HEAD_DIM), lambda h: (0, h))
    key = pl.BlockSpec((length, HEAD_DIM), lambda h: (0, h // steps))
    value = pl.BlockSpec((length, HEAD_DIM), lambda h: (0, KV_HEADS + h // steps))
    column = pl.BlockSpec((rows, 1), lambda h: (0, 0))
    stat = pl.BlockSpec((many, rows, 1), lambda h: (h, 0, 0))
    return head, key, value, column, stat


def attention_forward(queries, pair, lo, hi):
    rows, length = queries.shape[0], pair.shape[0]
    many = heads_per_step(length)
    head, key, value, column, stat = attention_specs(rows, length, many)
    return pl.pallas_call(
        forward_kernel,
        grid=(HEADS // many,),
        in_specs=[head, key, value, column, column],
        out_specs=[head, stat],
        out_shape=[shape((rows, WIDTH), BF), shape((HEADS, rows, 1), F32)],
        compiler_params=params(),
        cost_estimate=cost(4 * rows * length * WIDTH, 4 * length * KV_WIDTH + 4 * rows * WIDTH, rows * length * HEADS),
        name="attention_forward",
    )(queries, pair, pair, lo, hi)


def backward_kernel(
    core_ref, q_ref, k_ref, v_ref, g_ref, lo_ref, hi_ref, logsum_ref, cos_ref, sin_ref, cosq_ref, sinq_ref,
    normed_ref, mixed_ref, branch_ref, dq_ref, dkv_ref, keep_ref, send_ref, dk_sum, dv_sum, turned_ref,
):
    step = pl.program_id(0)
    many = logsum_ref.shape[0]
    group = step // (GROUP // many)
    member = lax.rem(step, GROUP // many)

    @pl.when(step == 0)
    def _():
        turned_ref[...] = normed_ref[...].astype(F32).T.astype(BF)

    keys, values = k_ref[...], v_ref[...]
    allowed = allowed_of(lo_ref, hi_ref, q_ref.shape[0], keys.shape[0])
    dk, dv = None, None
    for i in range(many):
        queries, grads = q_ref[:, lanes_of(i)], g_ref[:, lanes_of(i)]
        scores = jnp.where(allowed, against(queries, keys) * FACTOR, NEGATIVE)
        shares = jnp.where(allowed, jnp.exp(scores - logsum_ref[i]), 0.0)
        grad_shares = against(grads, values)
        delta = jnp.sum(shares * grad_shares, axis=-1, keepdims=True)
        grad_scores = (shares * (grad_shares - delta)).astype(BF)
        dq = matmul(grad_scores, keys) * FACTOR
        dq_ref[:, lanes_of(i)] = rotate_back(dq, cosq_ref[...], sinq_ref[...]).astype(BF)
        dk_here = outer(grad_scores, queries) * FACTOR
        dv_here = outer(shares.astype(BF), grads)
        dk, dv = (dk_here, dv_here) if i == 0 else (dk + dk_here, dv + dv_here)

    @pl.when(member == 0)
    def _():
        dk_sum[...] = dk
        dv_sum[...] = dv

    @pl.when(member > 0)
    def _():
        dk_sum[...] += dk
        dv_sum[...] += dv

    @pl.when(member == GROUP // many - 1)
    def _():
        here = pl.multiple_of(group * HEAD_DIM, HEAD_DIM)
        there = pl.multiple_of(KV_WIDTH + group * HEAD_DIM, HEAD_DIM)
        dkv_ref[:, pl.ds(here, HEAD_DIM)] = rotate_back(dk_sum[...], cos_ref[...], sin_ref[...]).astype(BF)
        dkv_ref[:, pl.ds(there, HEAD_DIM)] = dv_sum[...].astype(BF)

    core = core_ref[0]
    width = many * HEAD_DIM
    columns = pl.ds(pl.multiple_of(step * width, HEAD_DIM), width)
    for lanes, ref, rows in runs_of(core, keep_ref, send_ref):
        ref[rows, columns] = matmul(turned_ref[lanes, :], dq_ref[...]).astype(BF)
    run = keep_ref.shape[0] // 2
    steps = run // width
    place = step // steps
    row = pl.multiple_of(place // 2 * run + lax.rem(step, steps) * width, HEAD_DIM)
    terms = outer(mixed_ref[...], branch_ref[...]).astype(BF)
    mine = lax.rem(place, 2) == core

    @pl.when(mine)
    def _():
        keep_ref[pl.ds(row, width), WIDTH:] = terms

    @pl.when(jnp.logical_not(mine))
    def _():
        send_ref[pl.ds(row, width), WIDTH:] = terms


def attention_backward(
    core, queries, pair, grads, lo, hi, logsum, cosine, sine, cosine_own, sine_own, normed, mixed, grad_branch
):
    rows, length = queries.shape[0], pair.shape[0]
    once = pl.Buffered(1)
    many = heads_per_step(length)
    head, key, value, column, stat = attention_specs(rows, length, many)
    fixed = lambda x: pl.BlockSpec(x.shape, lambda h: (0, 0), pipeline_mode=once)
    terms = shape((WIDTH // 2, 2 * WIDTH), BF)
    return pl.pallas_call(
        backward_kernel,
        grid=(HEADS // many,),
        in_specs=[SMEM, head, key, value, head, column, column, stat]
        + [fixed(x) for x in (cosine, sine, cosine_own, sine_own, normed)]
        + [head, fixed(grad_branch)],
        out_specs=[head, pl.BlockSpec((length, 2 * KV_WIDTH), lambda h: (0, 0))]
        + [pl.BlockSpec(terms.shape, lambda h: (0, 0))] * 2,
        out_shape=[shape((rows, WIDTH), BF), shape((length, 2 * KV_WIDTH), BF), terms, terms],
        scratch_shapes=[
            pltpu.VMEM((length, HEAD_DIM), F32),
            pltpu.VMEM((length, HEAD_DIM), F32),
            pltpu.VMEM((WIDTH, rows), BF),
        ],
        compiler_params=params(),
        cost_estimate=cost(10 * rows * length * WIDTH, 16 * length * KV_WIDTH, rows * length * HEADS),
        name="attention_backward",
    )(core, queries, pair, pair, grads, lo, hi, logsum, cosine, sine, cosine_own, sine_own, normed, mixed, grad_branch)


def branch_kernel(core_ref, mixed_ref, *refs):
    weights, (tokens_ref, gain_ref, middle_ref, first_ref, second_ref) = refs[:4], refs[4:]
    width = weights[0].shape[1]
    parts = [times(core_ref[0], mixed_ref, weights[2 * i], weights[2 * i + 1], width) for i in range(2)]
    middle = tokens_ref[...].astype(F32) + jnp.concatenate(parts, axis=1)
    middle_ref[...] = middle
    normed = (middle * inverse_rms(middle) * gain_ref[...]).astype(BF)
    half = first_ref.shape[1]
    for i in range(first_ref.shape[0]):
        first_ref[i] = normed[:half]
        second_ref[i] = normed[half:]


def branch(core, mixed, out_weight, tokens, gain, copies):
    rows = mixed.shape[0]
    return pl.pallas_call(
        branch_kernel,
        in_specs=[SMEM] + [VMEM] * 7,
        out_specs=[VMEM] * 3,
        out_shape=[shape((rows, WIDTH), F32)] + [shape((copies, rows // 2, WIDTH), BF)] * 2,
        compiler_params=params(),
        cost_estimate=cost(2 * rows * WIDTH * WIDTH, 2 * WIDTH * WIDTH),
        name="branch",
    )(core, mixed, *out_weight, tokens, gain)


def mlp_kernel(
    near_ref, other_ref, cot_near_ref, cot_other_ref, gate_ref, up_ref, down_ref,
    hidden_ref, grad_gate_ref, grad_up_ref, back_near_ref, back_other_ref, forth_near_ref, forth_other_ref,
):
    rows = near_ref.shape[0]
    tokens = jnp.concatenate([near_ref[...], other_ref[...]], axis=0)
    cotangent = jnp.concatenate([cot_near_ref[...], cot_other_ref[...]], axis=0)
    gate = matmul(tokens, gate_ref[...])
    upper = matmul(tokens, up_ref[...])
    grad_hidden = against(cotangent, down_ref[...])
    logistic = 1.0 / (1.0 + jnp.exp(-gate))
    silu = gate * logistic
    hidden = (silu * upper).astype(BF)
    hidden_ref[...] = hidden
    grad_gate = (grad_hidden * upper * logistic * (1.0 + gate * (1.0 - logistic))).astype(BF)
    grad_upper = (grad_hidden * silu).astype(BF)
    grad_gate_ref[...] = grad_gate
    grad_up_ref[...] = grad_upper
    back = (against(grad_gate, gate_ref[...]) + against(grad_upper, up_ref[...])).astype(BF)
    back_near_ref[...] = back[:rows]
    back_other_ref[...] = back[rows:]
    forth = matmul(hidden, down_ref[...]).astype(BF)
    forth_near_ref[...] = forth[:rows]
    forth_other_ref[...] = forth[rows:]


def mlp(near, other, cot_near, cot_other, gate_up, down):
    rows = 2 * near.shape[0]
    chunk = down.shape[0]
    part = lambda n: pl.BlockSpec((WIDTH, chunk), lambda i: (0, n))
    made = [shape((rows, chunk), BF)] * 3 + [shape(near.shape, BF)] * 4
    return pl.pallas_call(
        mlp_kernel,
        grid=(1,),
        in_specs=[whole(near)] * 4 + [part(0), part(1), whole(down)],
        out_specs=[whole(x) for x in made],
        out_shape=made,
        compiler_params=params(),
        cost_estimate=cost(12 * rows * WIDTH * chunk, 6 * WIDTH * chunk + 14 * rows * WIDTH, rows * chunk),
        name="mlp",
    )(near, other, cot_near, cot_other, gate_up, gate_up, down)


def outer_kernel(*refs, counts):
    blocks, position = [], 0
    for count in counts:
        blocks.append(jnp.concatenate([ref[...] for ref in refs[position:position + count]], axis=0))
        position += count
    for right, out_ref in zip(blocks[1:], refs[position:]):
        out_ref[...] = outer(blocks[0], right).astype(BF)


def outer_blocks(lefts, rights, name):
    depth = sum(x.shape[0] for x in lefts)
    width = lefts[0].shape[1]
    across = [blocks[0].shape[1] for blocks in rights]
    tile = 384 if width % 384 == 0 else width
    flat = [x for blocks in rights for x in blocks]
    return pl.pallas_call(
        functools.partial(outer_kernel, counts=(len(lefts), *map(len, rights))),
        grid=(width // tile,),
        in_specs=[pl.BlockSpec((x.shape[0], tile), lambda i: (0, i)) for x in lefts]
        + [pl.BlockSpec(x.shape, lambda i: (0, 0), pipeline_mode=pl.Buffered(1)) for x in flat],
        out_specs=[pl.BlockSpec((tile, n), lambda i: (i, 0)) for n in across],
        out_shape=[shape((width, n), BF) for n in across],
        compiler_params=params(),
        cost_estimate=cost(2 * depth * width * sum(across), 2 * (depth + width) * (width + sum(across))),
        name=name,
    )(*lefts, *flat)


def outer_by_core_kernel(core_ref, *refs, counts):
    outer_kernel(*refs, counts=counts)


def outer_by_core(core, lefts, rights, name):
    depth = sum(x.shape[0] for x in lefts)
    width = lefts[0].shape[1]
    across = [blocks[0].shape[1] for blocks in rights]
    tile = width // 4
    flat = [x for blocks in rights for x in blocks]
    return pl.pallas_call(
        functools.partial(outer_by_core_kernel, counts=(len(lefts), *map(len, rights))),
        grid_spec=pltpu.PrefetchScalarGridSpec(
            num_scalar_prefetch=1,
            grid=(4,),
            in_specs=[
                pl.BlockSpec((x.shape[0], tile), lambda i, c: (0, 2 * lax.rem(i, 2) + (c[0] ^ lax.div(i, 2))))
                for x in lefts
            ]
            + [pl.BlockSpec(x.shape, lambda i, c: (0, 0), pipeline_mode=pl.Buffered(1)) for x in flat],
            out_specs=[pl.BlockSpec((tile, n), lambda i, c: (i, 0)) for n in across],
        ),
        out_shape=[shape((width, n), BF) for n in across],
        compiler_params=params(),
        cost_estimate=cost(2 * depth * width * sum(across), 2 * (depth + width) * (width + sum(across))),
        name=name,
    )(core, *lefts, *flat)


def middle_kernel(
    core_ref, first_ref, middle_ref, cotangent_ref, gain_ref, *refs
):
    weights, second, (grad_ref, branch_ref, mixed_ref, norm_ref) = refs[:4], refs[4:-4], refs[-4:]
    total = jnp.concatenate(
        [jnp.sum(first_ref[...].astype(F32), axis=0), sum(ref[...].astype(F32) for ref in second)], axis=0
    )
    middle = middle_ref[...]
    scale = inverse_rms(middle)
    norm_ref[...] = jnp.sum(total * middle * scale, axis=0, keepdims=True)
    weighted = total * gain_ref[...]
    grad = (
        cotangent_ref[...].astype(F32)
        + scale * weighted
        - middle * (scale * scale * scale) * jnp.mean(weighted * middle, axis=-1, keepdims=True)
    )
    grad_ref[...] = grad
    low = grad.astype(BF)
    branch_ref[...] = low
    width = weights[0].shape[1]
    core = core_ref[0]
    for first, second in zip(runs_of(core, *weights[:2]), runs_of(core, *weights[2:])):
        lanes, ref, rows = first
        mixed_ref[:, lanes] = (
            against(low[:, :width], ref[rows, :]) + against(low[:, width:], second[1][rows, :])
        ).astype(BF)


def middle_back(core, terms, middle, cotangent, gain, out_weight):
    rows = middle.shape[0]
    return pl.pallas_call(
        middle_kernel,
        in_specs=[SMEM] + [VMEM] * (8 + len(terms[1])),
        out_specs=[VMEM] * 4,
        out_shape=[shape((rows, WIDTH), F32), shape((rows, WIDTH), BF), shape((rows, WIDTH), BF), shape((1, WIDTH), F32)],
        compiler_params=params(),
        cost_estimate=cost(2 * rows * WIDTH * WIDTH, 2 * WIDTH * WIDTH + 20 * rows * WIDTH),
        name="middle_back",
    )(core, terms[0], middle, cotangent, gain, *out_weight, *terms[1])


def tokens_kernel(
    core_ref, grads_ref, left_ref, left_other_ref, right_ref, right_other_ref, tokens_ref, gain_ref, middle_ref,
    out_ref, norm_ref, bias_ref, total_ref,
):
    grads = grads_ref[...]
    bias_ref[...] = jnp.sum(grads.astype(F32), axis=0, keepdims=True)
    core = core_ref[0]
    for first, second in zip(runs_of(core, left_ref, left_other_ref), runs_of(core, right_ref, right_other_ref)):
        lanes, ref, rows = first
        total_ref[:, lanes] = against(grads[:, :LEFT], ref[rows, :]) + against(
            grads[:, LEFT:], second[1][rows, :QKV - LEFT]
        )
    grad_normed = total_ref[...]
    inputs = tokens_ref[...].astype(F32)
    scale = inverse_rms(inputs)
    norm_ref[...] = jnp.sum(grad_normed * inputs * scale, axis=0, keepdims=True)
    weighted = grad_normed * gain_ref[...]
    out_ref[...] = (
        middle_ref[...]
        + scale * weighted
        - inputs * (scale * scale * scale) * jnp.mean(weighted * inputs, axis=-1, keepdims=True)
    )


def tokens_back(core, grads, left, right, tokens, gain, middle):
    rows = tokens.shape[0]
    return pl.pallas_call(
        tokens_kernel,
        in_specs=[SMEM] + [VMEM] * 8,
        out_specs=[VMEM] * 3,
        out_shape=[shape((rows, WIDTH), F32), shape((1, WIDTH), F32), shape((1, QKV), F32)],
        scratch_shapes=[pltpu.VMEM((rows, WIDTH), F32)],
        compiler_params=params(),
        cost_estimate=cost(2 * rows * WIDTH * QKV, 2 * WIDTH * QKV + 12 * rows * WIDTH),
        name="tokens_back",
    )(core, grads, *left, *right, tokens, gain, middle)


def gather(value, axis):
    return lax.all_gather(value, axis, axis=0, tiled=True)


def scatter_sum(value, axis):
    return lax.psum_scatter(value, axis, scatter_dimension=0, tiled=True)


def swap(value, axis):
    return lax.all_to_all(value, axis, 0, 0, tiled=True)


def hop(value, axis, size=2, flip=1):
    return lax.ppermute(value, axis, [(i, i ^ flip) for i in range(size)])


def after(value, *earlier):
    return lax.optimization_barrier((value, *earlier))[0]


def together(*values):
    return lax.optimization_barrier(values)


def gather_near(value, nz):
    copies = jnp.broadcast_to(value[None], (nz, *value.shape)).reshape(-1, value.shape[1])
    return swap(copies, "z").reshape(nz, *value.shape)


def share_near(copies):
    return swap(copies.reshape(-1, copies.shape[2]), "z").reshape(copies.shape)


def add_low(left, right):
    return (left.astype(F32) + right.astype(F32)).astype(BF)


def exchange_near(blocks, nz, own_z):
    out = [lax.dynamic_index_in_dim(blocks, own_z, 0, keepdims=False)]
    for flip in range(1, nz):
        out.append(hop(lax.dynamic_index_in_dim(blocks, own_z ^ flip, 0, keepdims=False), "z", nz, flip))
    return out


def add_up(blocks):
    total = blocks[0].astype(F32)
    for block in blocks[1:]:
        total = total + block.astype(F32)
    return total


def pair(own, other, bit, axis):
    first, second = jnp.where(bit == 0, own, other), jnp.where(bit == 0, other, own)
    return jnp.stack([first, second], axis=axis)


def gather_z(value, nz, own_z):
    blocks = jnp.stack([value] + [hop(value, "z", nz, j) for j in range(1, nz)])
    return jnp.concatenate([lax.dynamic_slice_in_dim(blocks, own_z ^ j, 1) for j in range(nz)], axis=0)


def halve(value, axis, flip, size, bit, dim):
    keep = lax.dynamic_index_in_dim(value, bit, dim, keepdims=False)
    send = lax.dynamic_index_in_dim(value, 1 - bit, dim, keepdims=False)
    return add_low(keep, hop(send, axis, size, flip))


def sum_all(value, seq, nz):
    for axis, size in (("seq", seq), ("y", 2), ("z", nz)):
        flip = 1
        while flip < size:
            value = value + hop(value, axis, size, flip)
            flip *= 2
    return value


def body(
    tokens,
    segments,
    w_query,
    b_query,
    w_key,
    b_key,
    w_value,
    b_value,
    w_out,
    norm_attn,
    w_gate,
    w_up,
    w_down,
    norm_mlp,
    cotangent,
    *,
    seq,
    ctx,
):
    rows = tokens.shape[0]
    half = rows // 2
    nz = ctx // 2
    devices = seq * ctx
    share = w_query.shape[0]
    vshare = b_value.shape[0]
    run = w_down.shape[0]
    unit = LANES // math.gcd(LANES, seq)
    padded = -(-run // unit) * unit
    ident = segments[0]
    length = ident.shape[0]
    own_z, own_y, place = lax.axis_index("z"), lax.axis_index("y"), lax.axis_index("seq")
    index = 2 * own_z + own_y

    small = jnp.stack([norm_attn, norm_mlp, b_query, jnp.pad(b_value, (0, share - vshare))], axis=1)
    small = jnp.pad(small, ((0, 0), (0, LANES - 4)))
    projections = jnp.concatenate([w_query, w_key, w_value, small], axis=1)
    x, core = place // 2, place % 2
    over = lambda v, axis: hop(v, "seq", seq, 2) if axis == "x" else hop(v, "seq", seq, 1) if axis == "core" else hop(v, "y")
    flat = lambda v: v.reshape(2 * ctx * share, v.shape[-1])
    cuts = [slice(i * half, (i + 1) * half) for i in range(2)]
    count = nz * half
    cosine, sine = rope_tables(jnp.arange(length, dtype=jnp.int32) - ident)
    offset = index * rows
    hi = (offset + jnp.arange(rows, dtype=jnp.int32))[:, None]
    lo = lax.dynamic_slice_in_dim(ident, offset, rows)[:, None]
    tables = [cosine, sine] + [lax.dynamic_slice_in_dim(x, offset, rows) for x in (cosine, sine)] + [lo, hi]
    turned = columns_out(w_gate, w_up, seq, ctx, run, padded).reshape(ctx * share, -1)
    near = gather_near(after(projections, turned), nz)
    turned = swap(after(turned, near), CTX)
    left, right = near[:, :, :LEFT], near[:, :, LEFT:]
    left_got, right_got, near, tables = together(
        over(left, "y"), over(right, "x"), gather_z(after(w_out, near), nz, own_z), tables
    )
    left, right = pair(left, left_got, own_y, 1), pair(right, right_got, x, 0)
    out_left, out_right = near[:, :, :WIDTH // 2], near[:, :, WIDTH // 2:]
    left_got, right_got, out_left_got, out_right_got = together(
        over(left, "x"), over(right, "y"), over(out_left, "y"), over(out_right, "x")
    )
    left, right = flat(pair(left, left_got, x, 0)), flat(pair(right, right_got, own_y, 2))
    out_left, out_right = pair(out_left, out_left_got, own_y, 1), pair(out_right, out_right_got, x, 0)
    left_got, right_got, out_left_got, out_right_got = together(
        over(left, "core"), over(right, "core"), over(out_left, "x"), over(out_right, "y")
    )
    left, right = (left, left_got), (right, right_got)
    out_left, out_right = flat(pair(out_left, out_left_got, x, 0)), flat(pair(out_right, out_right_got, own_y, 2))
    out_weight = (out_left, over(out_left, "core"), out_right, over(out_right, "core"))
    down = jnp.pad(w_down, ((0, padded - run), (0, 0)))
    down = gather(down, "seq")
    gate_up = gather(after(turned, left_got), "seq")
    cotangent_low = after(cotangent, turned)
    cot_near = [gather_near(cotangent_low[cuts[0]], nz).reshape(count, WIDTH)]
    cosine, sine, cosine_own, sine_own, lo, hi = tables
    core = core.astype(jnp.int32)[None]
    vectors = vectors_of(core, right, 8)
    attn_gain, mlp_gain, query_bias = vectors[0:1], vectors[1:2], vectors[2:3]
    value_bias = vectors[3].reshape(devices, share)[:, :vshare].reshape(1, KV_WIDTH)

    normed, queries, kv = project(
        core, tokens, left, right, attn_gain, query_bias, b_key.astype(F32)[None], value_bias, cosine_own, sine_own, nz
    )
    near = share_near(after(kv, cot_near[0]))
    cot_near.append(gather_near(after(cotangent, near)[cuts[1]], nz).reshape(count, WIDTH))
    other = hop(near, "y")
    cot_other = [hop(after(x, other), "y") for x in cot_near]
    kv = pair(near, other, own_y, 1).reshape(length, 2 * KV_WIDTH)
    mixed, logsum = attention_forward(queries, kv, lo, hi)
    mixed, out_weight, cot_other[0] = together(mixed, out_weight, cot_other[0])
    middle, *copies = branch(core, mixed, out_weight, tokens, mlp_gain, nz)

    copies[1] = after(copies[1], cot_near[1], cot_other[1])
    x_near = [share_near(x).reshape(count, WIDTH) for x in copies]
    x_other = [hop(x, "y") for x in x_near]
    runs = [mlp(x_near[0], x_other[0], cot_near[0], cot_other[0], gate_up, down)]
    x_other[1] = after(x_other[1], *runs[0])
    runs.append(mlp(x_near[1], x_other[1], cot_near[1], cot_other[1], gate_up, down))
    hidden, grads_gate, grads_up, back_near, back_other, forth_near, forth_other = zip(*runs)
    sums = []
    for i in range(2):
        sums.append(add_low(back_near[i], hop(after(back_other[i], *sums), "y")))
    far = [swap(sums[0], "z").reshape(nz, half, WIDTH), exchange_near(sums[1].reshape(nz, half, WIDTH), nz, own_z)]
    x_all = [x_near[0], x_other[0], x_near[1], x_other[1]]
    cots = [cot_near[0], cot_other[0], cot_near[1], cot_other[1]]
    forth_got = [hop(after(x, *sums), "y") for x in forth_other]
    grads_gate, grads_up = after((grads_gate, grads_up), far, forth_got[0])
    grad_w_gate, grad_w_up = outer_by_core(core, x_all, [grads_gate, grads_up], "gate_up_grads")
    grads_two = [add_low(v[:WIDTH // 2], hop(v[WIDTH // 2:], "seq", seq, 1)) for v in (grad_w_gate, grad_w_up)]

    grad_middle, grad_branch, grad_mixed, norm_mlp_sum = middle_back(core, far, middle, cotangent, mlp_gain, out_weight)
    grad_mixed, forth_got, grads_two = together(grad_mixed, forth_got, grads_two)
    pairs = [[n, n + 2] for n in range(2)]
    grad_w_gate, grad_w_up = (
        lax.psum_scatter(v, "seq", scatter_dimension=0, axis_index_groups=pairs, tiled=True) for v in grads_two
    )
    dq, dkv, keep, send = attention_backward(
        core, queries, kv, grad_mixed, lo, hi, logsum, cosine, sine, cosine_own, sine_own, normed, mixed, grad_branch
    )
    forth = jnp.concatenate(
        [add_low(x, y).reshape(nz, half, WIDTH) for x, y in zip(forth_near, forth_got)], axis=1
    )
    forth = exchange_near(forth, nz, own_z)
    terms = swap(dkv, CTX).reshape(ctx, rows, 2 * KV_WIDTH)
    terms = jnp.sum(terms.astype(F32), axis=0).astype(BF)

    over_core = lambda v: halve(v, "seq", 1, seq, place % 2, 1)
    over_x = lambda v: halve(v, "seq", 2, seq, place // 2, 0)
    over_y = lambda v: halve(v, "y", 1, 2, own_y, v.ndim - 3)
    sides = add_low(keep, over(send, "core")).reshape(2, nz, 2, share, -1)
    grad_query, grad_out = over_x(sides[..., :WIDTH]), over_y(sides[..., WIDTH:])
    (grad_w_down,) = outer_blocks(after(hidden, sides), [cots], "down_grads")
    grad_w_down = scatter_sum(grad_w_down, "seq")[:run].astype(F32)
    grad_w_gate = swap(after(grad_w_gate, terms), CTX).reshape(ctx, share, -1)
    (grad_pair,) = outer_blocks([normed], [[after(terms, grad_out, grad_query)]], "pair_grads")
    grad_tokens, norm_attn_sum, bias = tokens_back(
        core, jnp.concatenate([dq, after(terms, grad_pair)], axis=1), left, right, tokens, attn_gain, grad_middle
    )
    grad_pair, bias, forth, grad_w_gate = together(grad_pair, bias, forth, grad_w_gate)
    grad_w_up = swap(after(grad_w_up, grad_w_gate), CTX).reshape(ctx, share, -1)
    grad_pair = over_core(grad_pair.reshape(2, 2, nz, 2, share, -1))
    grad_out, grad_query = over_x(grad_out), over_y(grad_query)
    grad_w_up, grad_out, grad_query, grad_pair = together(grad_w_up, grad_out, grad_query, grad_pair)
    side = add_up(exchange_near(jnp.concatenate([grad_out, grad_query], axis=2), nz, own_z))
    grad_pair = add_up(exchange_near(over_y(over_x(grad_pair)), nz, own_z))
    grad_w_out, grad_w_query = side[:, :WIDTH], side[:, WIDTH:]
    grad_w_key, grad_w_value = grad_pair[:, :KV_WIDTH], grad_pair[:, KV_WIDTH:]
    output = middle + add_up(forth)
    grad_w_gate, grad_w_up = columns_in(grad_w_gate, grad_w_up, seq, ctx, run, padded)

    sums = sum_all(jnp.concatenate([norm_attn_sum, norm_mlp_sum, bias], axis=1), seq, nz)[0]
    number = place * ctx + index
    mine = lambda start, size: lax.dynamic_slice_in_dim(sums, start + number * size, size)
    g_norm_attn, g_norm_mlp, g_b_query = (mine(n * WIDTH, share) for n in range(3))
    g_b_key = sums[3 * WIDTH:3 * WIDTH + KV_WIDTH]
    g_b_value = mine(3 * WIDTH + KV_WIDTH, vshare)
    return (
        output,
        grad_tokens,
        grad_w_query,
        g_b_query,
        grad_w_key,
        g_b_key,
        grad_w_value,
        g_b_value,
        grad_w_out,
        g_norm_attn,
        grad_w_gate,
        grad_w_up,
        grad_w_down,
        g_norm_mlp,
    )


def solution(mesh):
    seq, ctx = mesh.shape["seq"], mesh.shape["ctx"]
    rows2, rows1 = P(ALL, None), P(ALL)
    return jax.shard_map(
        functools.partial(body, seq=seq, ctx=ctx),
        mesh=Mesh(mesh.devices.reshape(seq, ctx // 2, 2), ALL),
        in_specs=(
            rows2,
            P("seq", None),
            rows2,
            rows1,
            rows2,
            P(),
            rows2,
            rows1,
            rows2,
            rows1,
            rows2,
            rows2,
            rows2,
            rows1,
            rows2,
        ),
        out_specs=(
            rows2,
            rows2,
            rows2,
            rows1,
            rows2,
            P(),
            rows2,
            rows1,
            rows2,
            rows1,
            rows2,
            rows2,
            rows2,
            rows1,
        ),
        check_vma=False,
    )
```

```python
import functools
import math

import jax
import jax.numpy as jnp
from jax import lax
from jax.experimental import pallas as pl
from jax.experimental.pallas import tpu as pltpu
from jax.sharding import Mesh
from jax.sharding import PartitionSpec as P

HEADS = 12
KV_HEADS = 2
HEAD_DIM = 128
WIDTH = 1536
KV_WIDTH = 256
GROUP = HEADS // KV_HEADS
QKV = WIDTH + 2 * KV_WIDTH
LANES = 128

EPS = 1e-06
THETA = 1000000.0
NEGATIVE = -1e30
FACTOR = HEAD_DIM ** (-0.5)
VMEM_LIMIT = 58 * 1024 * 1024

CTX = ("z", "y")
ALL = ("seq", "z", "y")
BF = jnp.bfloat16
F32 = jnp.float32
LEFT = 1024
VMEM = pl.BlockSpec(memory_space=pltpu.VMEM)
SMEM = pl.BlockSpec(memory_space=pltpu.SMEM)


def shape(dims, kind):
    return jax.ShapeDtypeStruct(dims, kind)


def cost(flops, nbytes, exps=0):
    return pl.CostEstimate(flops=int(flops), bytes_accessed=int(nbytes), transcendentals=int(exps))


def whole(value):
    return pl.BlockSpec(value.shape, lambda i: (0,) * value.ndim)


def params():
    return pltpu.CompilerParams(vmem_limit_bytes=VMEM_LIMIT)


def inverse_rms(values):
    return lax.rsqrt(jnp.mean(values * values, axis=-1, keepdims=True) + EPS)


def matmul(left, right):
    return jnp.dot(left, right, preferred_element_type=F32)


def against(left, weight):
    return lax.dot_general(left, weight, (((1,), (1,)), ((), ())), preferred_element_type=F32)


def outer(left, right):
    return lax.dot_general(left, right, (((0,), (0,)), ((), ())), preferred_element_type=F32)


def rope_tables(positions):
    half = HEAD_DIM // 2
    freqs = THETA ** (-(2.0 * jnp.arange(half, dtype=F32)) / HEAD_DIM)
    angles = positions.astype(F32)[:, None] * freqs[None, :]
    cosine, sine = jnp.cos(angles), jnp.sin(angles)
    return jnp.concatenate([cosine, cosine], axis=-1), jnp.concatenate([-sine, sine], axis=-1)


def rotate(head, cosine, sine):
    return head * cosine + pltpu.roll(head, HEAD_DIM // 2, 1) * sine


def rotate_back(head, cosine, sine):
    return head * cosine - pltpu.roll(head, HEAD_DIM // 2, 1) * sine


def columns_out_kernel(gate_ref, up_ref, out_ref, *, seq, ctx, run, padded):
    chunk = seq * padded
    rows = gate_ref.shape[0]
    blank = jnp.zeros((rows, padded - run), BF)
    for which, ref in enumerate((gate_ref, up_ref)):
        for part in range(ctx):
            pieces = []
            for place in range(seq):
                start = (place * ctx + part) * run
                pieces += [ref[:, start:start + run], blank]
            out_ref[part, :, which * chunk:(which + 1) * chunk] = jnp.concatenate(pieces, axis=1)


def columns_out(gate, up, seq, ctx, run, padded):
    rows = gate.shape[0]
    return pl.pallas_call(
        functools.partial(columns_out_kernel, seq=seq, ctx=ctx, run=run, padded=padded),
        in_specs=[VMEM, VMEM],
        out_specs=VMEM,
        out_shape=shape((ctx, rows, 2 * seq * padded), BF),
        compiler_params=params(),
        cost_estimate=cost(0, 4 * gate.size * 2),
        name="columns_out",
    )(gate, up)


def columns_in_kernel(gate_in_ref, up_in_ref, gate_ref, up_ref, *, seq, ctx, run, padded):
    for in_ref, ref in ((gate_in_ref, gate_ref), (up_in_ref, up_ref)):
        pieces = []
        for place in range(seq):
            for part in range(ctx):
                pieces.append(in_ref[part, :, place * padded:place * padded + run])
        ref[...] = jnp.concatenate(pieces, axis=1).astype(F32)


def columns_in(gate, up, seq, ctx, run, padded):
    rows = gate.shape[1]
    return pl.pallas_call(
        functools.partial(columns_in_kernel, seq=seq, ctx=ctx, run=run, padded=padded),
        in_specs=[VMEM, VMEM],
        out_specs=[VMEM, VMEM],
        out_shape=[shape((rows, seq * ctx * run), F32)] * 2,
        compiler_params=params(),
        cost_estimate=cost(0, gate.size * 12),
        name="columns_in",
    )(gate, up)


def runs_of(core, own_ref, other_ref):
    run = own_ref.shape[0] // 2
    for x in range(2):
        for flip, ref in enumerate((own_ref, other_ref)):
            start = pl.multiple_of((2 * x + (core ^ flip)) * run, LANES)
            yield pl.ds(start, run), ref, slice(x * run, (x + 1) * run)


def times(core, left_ref, own_ref, other_ref, width):
    total = None
    for lanes, ref, rows in runs_of(core, own_ref, other_ref):
        term = matmul(left_ref[:, lanes], ref[rows, :width])
        total = term if total is None else total + term
    return total


def project_kernel(
    core_ref, tokens_ref, left_ref, left_other_ref, right_ref, right_other_ref,
    gain_ref, qbias_ref, kbias_ref, vbias_ref, cos_ref, sin_ref,
    normed_ref, query_ref, pair_out_ref,
):
    core = core_ref[0]
    inputs = tokens_ref[...].astype(F32)
    normed_ref[...] = (inputs * inverse_rms(inputs) * gain_ref[...]).astype(BF)
    left = times(core, normed_ref, left_ref, left_other_ref, LEFT)
    right = times(core, normed_ref, right_ref, right_other_ref, QKV - LEFT)
    query = jnp.concatenate([left, right[:, :WIDTH - LEFT]], axis=1) + qbias_ref[...]
    pair = right[:, WIDTH - LEFT:]
    key = pair[:, :KV_WIDTH] + kbias_ref[...]
    cosine, sine = cos_ref[...], sin_ref[...]
    for h in range(HEADS):
        lanes = slice(h * HEAD_DIM, (h + 1) * HEAD_DIM)
        query_ref[:, lanes] = rotate(query[:, lanes], cosine, sine).astype(BF)
    for g in range(KV_HEADS):
        lanes = slice(g * HEAD_DIM, (g + 1) * HEAD_DIM)
        pair_out_ref[:, lanes] = rotate(key[:, lanes], cosine, sine).astype(BF)
    pair_out_ref[:, KV_WIDTH:] = (pair[:, KV_WIDTH:] + vbias_ref[...]).astype(BF)


def project(core, tokens, left, right, gain, qbias, kbias, vbias, cosine, sine):
    rows = tokens.shape[0]
    return pl.pallas_call(
        project_kernel,
        in_specs=[SMEM] + [VMEM] * 11,
        out_specs=[VMEM] * 3,
        out_shape=[shape((rows, WIDTH), BF), shape((rows, WIDTH), BF), shape((rows, 2 * KV_WIDTH), BF)],
        compiler_params=params(),
        cost_estimate=cost(2 * rows * WIDTH * QKV, 2 * WIDTH * QKV + 6 * rows * WIDTH),
        name="project",
    )(core, tokens, *left, *right, gain, qbias, kbias, vbias, cosine, sine)


def vectors_kernel(core_ref, own_ref, other_ref, out_ref):
    for lanes, ref, rows in runs_of(core_ref[0], own_ref, other_ref):
        out_ref[:, lanes] = ref[rows, :].astype(F32).T[:out_ref.shape[0]]


def vectors_of(core, right, count):
    depth, width = right[0].shape
    block = pl.BlockSpec((depth, LANES), lambda i: (0, width // LANES - 1))
    return pl.pallas_call(
        vectors_kernel,
        grid=(1,),
        in_specs=[SMEM, block, block],
        out_specs=pl.BlockSpec((count, 2 * depth), lambda i: (0, 0)),
        out_shape=shape((count, 2 * depth), F32),
        compiler_params=params(),
        cost_estimate=cost(0, 4 * depth * LANES),
        name="vectors",
    )(core, *right)


def allowed_of(lo_ref, hi_ref, rows, length):
    places = lax.broadcasted_iota(jnp.int32, (rows, length), 1)
    return (places >= lo_ref[...]) & (places <= hi_ref[...])


def heads_per_step(length):
    return 3 if length <= 1024 else 1


def lanes_of(i):
    return slice(i * HEAD_DIM, (i + 1) * HEAD_DIM)


def forward_kernel(q_ref, k_ref, v_ref, lo_ref, hi_ref, mixed_ref, logsum_ref):
    keys, values = k_ref[...], v_ref[...]
    allowed = allowed_of(lo_ref, hi_ref, q_ref.shape[0], keys.shape[0])
    for i in range(logsum_ref.shape[0]):
        scores = jnp.where(allowed, against(q_ref[:, lanes_of(i)], keys) * FACTOR, NEGATIVE)
        top = jnp.max(scores, axis=-1, keepdims=True)
        weights = jnp.exp(scores - top)
        total = jnp.sum(weights, axis=-1, keepdims=True)
        shares = (weights * (1.0 / total)).astype(BF)
        mixed_ref[:, lanes_of(i)] = matmul(shares, values).astype(BF)
        logsum_ref[i] = top + jnp.log(total)


def attention_specs(rows, length, many):
    steps = GROUP // many
    head = pl.BlockSpec((rows, many * HEAD_DIM), lambda h: (0, h))
    key = pl.BlockSpec((length, HEAD_DIM), lambda h: (0, h // steps))
    value = pl.BlockSpec((length, HEAD_DIM), lambda h: (0, KV_HEADS + h // steps))
    column = pl.BlockSpec((rows, 1), lambda h: (0, 0))
    stat = pl.BlockSpec((many, rows, 1), lambda h: (h, 0, 0))
    return head, key, value, column, stat


def attention_forward(queries, pair, lo, hi):
    rows, length = queries.shape[0], pair.shape[0]
    many = heads_per_step(length)
    head, key, value, column, stat = attention_specs(rows, length, many)
    return pl.pallas_call(
        forward_kernel,
        grid=(HEADS // many,),
        in_specs=[head, key, value, column, column],
        out_specs=[head, stat],
        out_shape=[shape((rows, WIDTH), BF), shape((HEADS, rows, 1), F32)],
        compiler_params=params(),
        cost_estimate=cost(4 * rows * length * WIDTH, 4 * length * KV_WIDTH + 4 * rows * WIDTH, rows * length * HEADS),
        name="attention_forward",
    )(queries, pair, pair, lo, hi)


def backward_kernel(
    core_ref, q_ref, k_ref, v_ref, g_ref, lo_ref, hi_ref, logsum_ref, cos_ref, sin_ref, cosq_ref, sinq_ref,
    normed_ref, mixed_ref, branch_ref, dq_ref, dkv_ref, keep_ref, send_ref, dk_sum, dv_sum, turned_ref,
):
    step = pl.program_id(0)
    many = logsum_ref.shape[0]
    group = step // (GROUP // many)
    member = lax.rem(step, GROUP // many)

    @pl.when(step == 0)
    def _():
        turned_ref[...] = normed_ref[...].astype(F32).T.astype(BF)

    keys, values = k_ref[...], v_ref[...]
    allowed = allowed_of(lo_ref, hi_ref, q_ref.shape[0], keys.shape[0])
    dk, dv = None, None
    for i in range(many):
        queries, grads = q_ref[:, lanes_of(i)], g_ref[:, lanes_of(i)]
        scores = jnp.where(allowed, against(queries, keys) * FACTOR, NEGATIVE)
        shares = jnp.where(allowed, jnp.exp(scores - logsum_ref[i]), 0.0)
        grad_shares = against(grads, values)
        delta = jnp.sum(shares * grad_shares, axis=-1, keepdims=True)
        grad_scores = (shares * (grad_shares - delta)).astype(BF)
        dq = matmul(grad_scores, keys) * FACTOR
        dq_ref[:, lanes_of(i)] = rotate_back(dq, cosq_ref[...], sinq_ref[...]).astype(BF)
        dk_here = outer(grad_scores, queries) * FACTOR
        dv_here = outer(shares.astype(BF), grads)
        dk, dv = (dk_here, dv_here) if i == 0 else (dk + dk_here, dv + dv_here)

    @pl.when(member == 0)
    def _():
        dk_sum[...] = dk
        dv_sum[...] = dv

    @pl.when(member > 0)
    def _():
        dk_sum[...] += dk
        dv_sum[...] += dv

    @pl.when(member == GROUP // many - 1)
    def _():
        here = pl.multiple_of(group * HEAD_DIM, HEAD_DIM)
        there = pl.multiple_of(KV_WIDTH + group * HEAD_DIM, HEAD_DIM)
        dkv_ref[:, pl.ds(here, HEAD_DIM)] = rotate_back(dk_sum[...], cos_ref[...], sin_ref[...]).astype(BF)
        dkv_ref[:, pl.ds(there, HEAD_DIM)] = dv_sum[...].astype(BF)

    core = core_ref[0]
    width = many * HEAD_DIM
    columns = pl.ds(pl.multiple_of(step * width, HEAD_DIM), width)
    for lanes, ref, rows in runs_of(core, keep_ref, send_ref):
        ref[rows, columns] = matmul(turned_ref[lanes, :], dq_ref[...]).astype(BF)
    run = keep_ref.shape[0] // 2
    steps = run // width
    place = step // steps
    row = pl.multiple_of(place // 2 * run + lax.rem(step, steps) * width, HEAD_DIM)
    terms = outer(mixed_ref[...], branch_ref[...]).astype(BF)
    mine = lax.rem(place, 2) == core

    @pl.when(mine)
    def _():
        keep_ref[pl.ds(row, width), WIDTH:] = terms

    @pl.when(jnp.logical_not(mine))
    def _():
        send_ref[pl.ds(row, width), WIDTH:] = terms


def attention_backward(
    core, queries, pair, grads, lo, hi, logsum, cosine, sine, cosine_own, sine_own, normed, mixed, grad_branch
):
    rows, length = queries.shape[0], pair.shape[0]
    once = pl.Buffered(1)
    many = heads_per_step(length)
    head, key, value, column, stat = attention_specs(rows, length, many)
    fixed = lambda x: pl.BlockSpec(x.shape, lambda h: (0, 0), pipeline_mode=once)
    terms = shape((WIDTH // 2, 2 * WIDTH), BF)
    return pl.pallas_call(
        backward_kernel,
        grid=(HEADS // many,),
        in_specs=[SMEM, head, key, value, head, column, column, stat]
        + [fixed(x) for x in (cosine, sine, cosine_own, sine_own, normed)]
        + [head, fixed(grad_branch)],
        out_specs=[head, pl.BlockSpec((length, 2 * KV_WIDTH), lambda h: (0, 0))]
        + [pl.BlockSpec(terms.shape, lambda h: (0, 0))] * 2,
        out_shape=[shape((rows, WIDTH), BF), shape((length, 2 * KV_WIDTH), BF), terms, terms],
        scratch_shapes=[
            pltpu.VMEM((length, HEAD_DIM), F32),
            pltpu.VMEM((length, HEAD_DIM), F32),
            pltpu.VMEM((WIDTH, rows), BF),
        ],
        compiler_params=params(),
        cost_estimate=cost(10 * rows * length * WIDTH, 16 * length * KV_WIDTH, rows * length * HEADS),
        name="attention_backward",
    )(core, queries, pair, pair, grads, lo, hi, logsum, cosine, sine, cosine_own, sine_own, normed, mixed, grad_branch)


def branch_kernel(core_ref, mixed_ref, *refs):
    weights, (tokens_ref, gain_ref, middle_ref, first_ref, second_ref) = refs[:4], refs[4:]
    width = weights[0].shape[1]
    parts = [times(core_ref[0], mixed_ref, weights[2 * i], weights[2 * i + 1], width) for i in range(2)]
    middle = tokens_ref[...].astype(F32) + jnp.concatenate(parts, axis=1)
    middle_ref[...] = middle
    normed = (middle * inverse_rms(middle) * gain_ref[...]).astype(BF)
    half = first_ref.shape[1]
    for i in range(first_ref.shape[0]):
        first_ref[i] = normed[:half]
        second_ref[i] = normed[half:]


def branch(core, mixed, out_weight, tokens, gain, copies):
    rows = mixed.shape[0]
    return pl.pallas_call(
        branch_kernel,
        in_specs=[SMEM] + [VMEM] * 7,
        out_specs=[VMEM] * 3,
        out_shape=[shape((rows, WIDTH), F32)] + [shape((copies, rows // 2, WIDTH), BF)] * 2,
        compiler_params=params(),
        cost_estimate=cost(2 * rows * WIDTH * WIDTH, 2 * WIDTH * WIDTH),
        name="branch",
    )(core, mixed, *out_weight, tokens, gain)


def mlp_kernel(
    near_ref, other_ref, cot_near_ref, cot_other_ref, gate_ref, up_ref, down_ref,
    hidden_ref, grad_gate_ref, grad_up_ref, back_near_ref, back_other_ref, forth_near_ref, forth_other_ref,
):
    rows = near_ref.shape[0]
    tokens = jnp.concatenate([near_ref[...], other_ref[...]], axis=0)
    cotangent = jnp.concatenate([cot_near_ref[...], cot_other_ref[...]], axis=0)
    gate = matmul(tokens, gate_ref[...])
    upper = matmul(tokens, up_ref[...])
    grad_hidden = against(cotangent, down_ref[...])
    logistic = 1.0 / (1.0 + jnp.exp(-gate))
    silu = gate * logistic
    hidden = (silu * upper).astype(BF)
    hidden_ref[...] = hidden
    grad_gate = (grad_hidden * upper * logistic * (1.0 + gate * (1.0 - logistic))).astype(BF)
    grad_upper = (grad_hidden * silu).astype(BF)
    grad_gate_ref[...] = grad_gate
    grad_up_ref[...] = grad_upper
    back = (against(grad_gate, gate_ref[...]) + against(grad_upper, up_ref[...])).astype(BF)
    back_near_ref[...] = back[:rows]
    back_other_ref[...] = back[rows:]
    forth = matmul(hidden, down_ref[...]).astype(BF)
    forth_near_ref[...] = forth[:rows]
    forth_other_ref[...] = forth[rows:]


def mlp(near, other, cot_near, cot_other, gate_up, down):
    rows = 2 * near.shape[0]
    chunk = down.shape[0]
    part = lambda n: pl.BlockSpec((WIDTH, chunk), lambda i: (0, n))
    made = [shape((rows, chunk), BF)] * 3 + [shape(near.shape, BF)] * 4
    return pl.pallas_call(
        mlp_kernel,
        grid=(1,),
        in_specs=[whole(near)] * 4 + [part(0), part(1), whole(down)],
        out_specs=[whole(x) for x in made],
        out_shape=made,
        compiler_params=params(),
        cost_estimate=cost(12 * rows * WIDTH * chunk, 6 * WIDTH * chunk + 14 * rows * WIDTH, rows * chunk),
        name="mlp",
    )(near, other, cot_near, cot_other, gate_up, gate_up, down)


def outer_kernel(*refs, counts):
    blocks, position = [], 0
    for count in counts:
        blocks.append(jnp.concatenate([ref[...] for ref in refs[position:position + count]], axis=0))
        position += count
    for right, out_ref in zip(blocks[1:], refs[position:]):
        out_ref[...] = outer(blocks[0], right).astype(BF)


def outer_blocks(lefts, rights, name):
    depth = sum(x.shape[0] for x in lefts)
    width = lefts[0].shape[1]
    across = [blocks[0].shape[1] for blocks in rights]
    tile = 384 if width % 384 == 0 else width
    flat = [x for blocks in rights for x in blocks]
    return pl.pallas_call(
        functools.partial(outer_kernel, counts=(len(lefts), *map(len, rights))),
        grid=(width // tile,),
        in_specs=[pl.BlockSpec((x.shape[0], tile), lambda i: (0, i)) for x in lefts]
        + [pl.BlockSpec(x.shape, lambda i: (0, 0), pipeline_mode=pl.Buffered(1)) for x in flat],
        out_specs=[pl.BlockSpec((tile, n), lambda i: (i, 0)) for n in across],
        out_shape=[shape((width, n), BF) for n in across],
        compiler_params=params(),
        cost_estimate=cost(2 * depth * width * sum(across), 2 * (depth + width) * (width + sum(across))),
        name=name,
    )(*lefts, *flat)


def outer_by_core_kernel(core_ref, *refs, counts):
    outer_kernel(*refs, counts=counts)


def outer_by_core(core, lefts, rights, name):
    depth = sum(x.shape[0] for x in lefts)
    width = lefts[0].shape[1]
    across = [blocks[0].shape[1] for blocks in rights]
    tile = width // 4
    flat = [x for blocks in rights for x in blocks]
    return pl.pallas_call(
        functools.partial(outer_by_core_kernel, counts=(len(lefts), *map(len, rights))),
        grid_spec=pltpu.PrefetchScalarGridSpec(
            num_scalar_prefetch=1,
            grid=(4,),
            in_specs=[
                pl.BlockSpec((x.shape[0], tile), lambda i, c: (0, 2 * lax.rem(i, 2) + (c[0] ^ lax.div(i, 2))))
                for x in lefts
            ]
            + [pl.BlockSpec(x.shape, lambda i, c: (0, 0), pipeline_mode=pl.Buffered(1)) for x in flat],
            out_specs=[pl.BlockSpec((tile, n), lambda i, c: (i, 0)) for n in across],
        ),
        out_shape=[shape((width, n), BF) for n in across],
        compiler_params=params(),
        cost_estimate=cost(2 * depth * width * sum(across), 2 * (depth + width) * (width + sum(across))),
        name=name,
    )(core, *lefts, *flat)


def middle_kernel(
    core_ref, first_ref, middle_ref, cotangent_ref, gain_ref, *refs
):
    weights, second, (grad_ref, branch_ref, mixed_ref, norm_ref) = refs[:4], refs[4:-4], refs[-4:]
    total = jnp.concatenate(
        [jnp.sum(first_ref[...].astype(F32), axis=0), sum(ref[...].astype(F32) for ref in second)], axis=0
    )
    middle = middle_ref[...]
    scale = inverse_rms(middle)
    norm_ref[...] = jnp.sum(total * middle * scale, axis=0, keepdims=True)
    weighted = total * gain_ref[...]
    grad = (
        cotangent_ref[...].astype(F32)
        + scale * weighted
        - middle * (scale * scale * scale) * jnp.mean(weighted * middle, axis=-1, keepdims=True)
    )
    grad_ref[...] = grad
    low = grad.astype(BF)
    branch_ref[...] = low
    width = weights[0].shape[1]
    core = core_ref[0]
    for first, second in zip(runs_of(core, *weights[:2]), runs_of(core, *weights[2:])):
        lanes, ref, rows = first
        mixed_ref[:, lanes] = (
            against(low[:, :width], ref[rows, :]) + against(low[:, width:], second[1][rows, :])
        ).astype(BF)


def middle_back(core, terms, middle, cotangent, gain, out_weight):
    rows = middle.shape[0]
    return pl.pallas_call(
        middle_kernel,
        in_specs=[SMEM] + [VMEM] * (8 + len(terms[1])),
        out_specs=[VMEM] * 4,
        out_shape=[shape((rows, WIDTH), F32), shape((rows, WIDTH), BF), shape((rows, WIDTH), BF), shape((1, WIDTH), F32)],
        compiler_params=params(),
        cost_estimate=cost(2 * rows * WIDTH * WIDTH, 2 * WIDTH * WIDTH + 20 * rows * WIDTH),
        name="middle_back",
    )(core, terms[0], middle, cotangent, gain, *out_weight, *terms[1])


def tokens_kernel(
    core_ref, grads_ref, left_ref, left_other_ref, right_ref, right_other_ref, tokens_ref, gain_ref, middle_ref,
    out_ref, norm_ref, bias_ref, total_ref,
):
    grads = grads_ref[...]
    bias_ref[...] = jnp.sum(grads.astype(F32), axis=0, keepdims=True)
    core = core_ref[0]
    for first, second in zip(runs_of(core, left_ref, left_other_ref), runs_of(core, right_ref, right_other_ref)):
        lanes, ref, rows = first
        total_ref[:, lanes] = against(grads[:, :LEFT], ref[rows, :]) + against(
            grads[:, LEFT:], second[1][rows, :QKV - LEFT]
        )
    grad_normed = total_ref[...]
    inputs = tokens_ref[...].astype(F32)
    scale = inverse_rms(inputs)
    norm_ref[...] = jnp.sum(grad_normed * inputs * scale, axis=0, keepdims=True)
    weighted = grad_normed * gain_ref[...]
    out_ref[...] = (
        middle_ref[...]
        + scale * weighted
        - inputs * (scale * scale * scale) * jnp.mean(weighted * inputs, axis=-1, keepdims=True)
    )


def tokens_back(core, grads, left, right, tokens, gain, middle):
    rows = tokens.shape[0]
    return pl.pallas_call(
        tokens_kernel,
        in_specs=[SMEM] + [VMEM] * 8,
        out_specs=[VMEM] * 3,
        out_shape=[shape((rows, WIDTH), F32), shape((1, WIDTH), F32), shape((1, QKV), F32)],
        scratch_shapes=[pltpu.VMEM((rows, WIDTH), F32)],
        compiler_params=params(),
        cost_estimate=cost(2 * rows * WIDTH * QKV, 2 * WIDTH * QKV + 12 * rows * WIDTH),
        name="tokens_back",
    )(core, grads, *left, *right, tokens, gain, middle)


def gather(value, axis):
    return lax.all_gather(value, axis, axis=0, tiled=True)


def scatter_sum(value, axis):
    return lax.psum_scatter(value, axis, scatter_dimension=0, tiled=True)


def swap(value, axis):
    return lax.all_to_all(value, axis, 0, 0, tiled=True)


def hop(value, axis, size=2, flip=1):
    return lax.ppermute(value, axis, [(i, i ^ flip) for i in range(size)])


def after(value, *earlier):
    return lax.optimization_barrier((value, *earlier))[0]


def together(*values):
    return lax.optimization_barrier(values)


def gather_near(value, nz):
    copies = jnp.broadcast_to(value[None], (nz, *value.shape)).reshape(-1, value.shape[1])
    return swap(copies, "z").reshape(nz, *value.shape)


def share_near(copies):
    return swap(copies.reshape(-1, copies.shape[2]), "z").reshape(copies.shape)


def add_low(left, right):
    return (left.astype(F32) + right.astype(F32)).astype(BF)


def exchange_near(blocks, nz, own_z):
    out = [lax.dynamic_index_in_dim(blocks, own_z, 0, keepdims=False)]
    for flip in range(1, nz):
        out.append(hop(lax.dynamic_index_in_dim(blocks, own_z ^ flip, 0, keepdims=False), "z", nz, flip))
    return out


def add_up(blocks):
    total = blocks[0].astype(F32)
    for block in blocks[1:]:
        total = total + block.astype(F32)
    return total


def pair(own, other, bit, axis):
    first, second = jnp.where(bit == 0, own, other), jnp.where(bit == 0, other, own)
    return jnp.stack([first, second], axis=axis)


def gather_z(value, nz, own_z):
    blocks = jnp.stack([value] + [hop(value, "z", nz, j) for j in range(1, nz)])
    return jnp.concatenate([lax.dynamic_slice_in_dim(blocks, own_z ^ j, 1) for j in range(nz)], axis=0)


def halve(value, axis, flip, size, bit, dim):
    keep = lax.dynamic_index_in_dim(value, bit, dim, keepdims=False)
    send = lax.dynamic_index_in_dim(value, 1 - bit, dim, keepdims=False)
    return add_low(keep, hop(send, axis, size, flip))


def sum_all(value, seq, nz):
    for axis, size in (("seq", seq), ("y", 2), ("z", nz)):
        flip = 1
        while flip < size:
            value = value + hop(value, axis, size, flip)
            flip *= 2
    return value


def body(
    tokens,
    segments,
    w_query,
    b_query,
    w_key,
    b_key,
    w_value,
    b_value,
    w_out,
    norm_attn,
    w_gate,
    w_up,
    w_down,
    norm_mlp,
    cotangent,
    *,
    seq,
    ctx,
):
    rows = tokens.shape[0]
    half = rows // 2
    nz = ctx // 2
    devices = seq * ctx
    share = w_query.shape[0]
    vshare = b_value.shape[0]
    run = w_down.shape[0]
    unit = LANES // math.gcd(LANES, seq)
    padded = -(-run // unit) * unit
    ident = segments[0]
    length = ident.shape[0]
    own_z, own_y, place = lax.axis_index("z"), lax.axis_index("y"), lax.axis_index("seq")
    index = 2 * own_z + own_y

    small = jnp.stack([norm_attn, norm_mlp, b_query, jnp.pad(b_value, (0, share - vshare))], axis=1)
    small = jnp.pad(small, ((0, 0), (0, LANES - 4)))
    projections = jnp.concatenate([w_query, w_key, w_value, small], axis=1)
    x, core = place // 2, place % 2
    over = lambda v, axis: hop(v, "seq", seq, 2) if axis == "x" else hop(v, "seq", seq, 1) if axis == "core" else hop(v, "y")
    flat = lambda v: v.reshape(2 * ctx * share, v.shape[-1])
    cuts = [slice(i * half, (i + 1) * half) for i in range(2)]
    count = nz * half
    cosine, sine = rope_tables(jnp.arange(length, dtype=jnp.int32) - ident)
    offset = index * rows
    hi = (offset + jnp.arange(rows, dtype=jnp.int32))[:, None]
    lo = lax.dynamic_slice_in_dim(ident, offset, rows)[:, None]
    tables = [cosine, sine] + [lax.dynamic_slice_in_dim(x, offset, rows) for x in (cosine, sine)] + [lo, hi]
    turned = columns_out(w_gate, w_up, seq, ctx, run, padded).reshape(ctx * share, -1)
    near = gather_near(after(projections, turned), nz)
    turned = swap(after(turned, near), CTX)
    left, right = near[:, :, :LEFT], near[:, :, LEFT:]
    left_got, right_got, near, tables = together(
        over(left, "y"), over(right, "x"), gather_z(after(w_out, near), nz, own_z), tables
    )
    left, right = pair(left, left_got, own_y, 1), pair(right, right_got, x, 0)
    out_left, out_right = near[:, :, :WIDTH // 2], near[:, :, WIDTH // 2:]
    left_got, right_got, out_left_got, out_right_got = together(
        over(left, "x"), over(right, "y"), over(out_left, "y"), over(out_right, "x")
    )
    left, right = flat(pair(left, left_got, x, 0)), flat(pair(right, right_got, own_y, 2))
    out_left, out_right = pair(out_left, out_left_got, own_y, 1), pair(out_right, out_right_got, x, 0)
    left_got, right_got, out_left_got, out_right_got = together(
        over(left, "core"), over(right, "core"), over(out_left, "x"), over(out_right, "y")
    )
    left, right = (left, left_got), (right, right_got)
    out_left, out_right = flat(pair(out_left, out_left_got, x, 0)), flat(pair(out_right, out_right_got, own_y, 2))
    out_weight = (out_left, over(out_left, "core"), out_right, over(out_right, "core"))
    down = jnp.pad(w_down, ((0, padded - run), (0, 0)))
    down = gather(down, "seq")
    gate_up = gather(after(turned, left_got), "seq")
    cotangent_low = after(cotangent, turned)
    cot_near = [gather_near(cotangent_low[cuts[0]], nz).reshape(count, WIDTH)]
    cosine, sine, cosine_own, sine_own, lo, hi = tables
    core = core.astype(jnp.int32)[None]
    vectors = vectors_of(core, right, 8)
    attn_gain, mlp_gain, query_bias = vectors[0:1], vectors[1:2], vectors[2:3]
    value_bias = vectors[3].reshape(devices, share)[:, :vshare].reshape(1, KV_WIDTH)

    normed, queries, kv = project(
        core, tokens, left, right, attn_gain, query_bias, b_key.astype(F32)[None], value_bias, cosine_own, sine_own
    )
    near = gather_z(kv, nz, own_z)
    cot_near.append(gather_near(after(cotangent, near)[cuts[1]], nz).reshape(count, WIDTH))
    other = hop(near, "y")
    cot_other = [hop(after(x, other), "y") for x in cot_near]
    kv = pair(near, other, own_y, 1).reshape(length, 2 * KV_WIDTH)
    mixed, logsum = attention_forward(queries, kv, lo, hi)
    mixed, out_weight, cot_other[0] = together(mixed, out_weight, cot_other[0])
    middle, *copies = branch(core, mixed, out_weight, tokens, mlp_gain, nz)

    copies[1] = after(copies[1], cot_near[1], cot_other[1])
    x_near = [share_near(x).reshape(count, WIDTH) for x in copies]
    x_other = [hop(x, "y") for x in x_near]
    runs = [mlp(x_near[0], x_other[0], cot_near[0], cot_other[0], gate_up, down)]
    x_other[1] = after(x_other[1], *runs[0])
    runs.append(mlp(x_near[1], x_other[1], cot_near[1], cot_other[1], gate_up, down))
    hidden, grads_gate, grads_up, back_near, back_other, forth_near, forth_other = zip(*runs)
    sums = []
    for i in range(2):
        sums.append(add_low(back_near[i], hop(after(back_other[i], *sums), "y")))
    far = [swap(sums[0], "z").reshape(nz, half, WIDTH), exchange_near(sums[1].reshape(nz, half, WIDTH), nz, own_z)]
    x_all = [x_near[0], x_other[0], x_near[1], x_other[1]]
    cots = [cot_near[0], cot_other[0], cot_near[1], cot_other[1]]
    forth_got = [hop(after(x, *sums), "y") for x in forth_other]
    grads_gate, grads_up = after((grads_gate, grads_up), far, forth_got[0])
    grad_w_gate, grad_w_up = outer_by_core(core, x_all, [grads_gate, grads_up], "gate_up_grads")
    grads_two = [add_low(v[:WIDTH // 2], hop(v[WIDTH // 2:], "seq", seq, 1)) for v in (grad_w_gate, grad_w_up)]

    grad_middle, grad_branch, grad_mixed, norm_mlp_sum = middle_back(core, far, middle, cotangent, mlp_gain, out_weight)
    grad_mixed, forth_got, grads_two = together(grad_mixed, forth_got, grads_two)
    pairs = [[n, n + 2] for n in range(2)]
    grad_w_gate, grad_w_up = (
        lax.psum_scatter(v, "seq", scatter_dimension=0, axis_index_groups=pairs, tiled=True) for v in grads_two
    )
    dq, dkv, keep, send = attention_backward(
        core, queries, kv, grad_mixed, lo, hi, logsum, cosine, sine, cosine_own, sine_own, normed, mixed, grad_branch
    )
    forth = jnp.concatenate(
        [add_low(x, y).reshape(nz, half, WIDTH) for x, y in zip(forth_near, forth_got)], axis=1
    )
    forth = exchange_near(forth, nz, own_z)
    terms = swap(dkv, CTX).reshape(ctx, rows, 2 * KV_WIDTH)
    terms = jnp.sum(terms.astype(F32), axis=0).astype(BF)

    over_core = lambda v: halve(v, "seq", 1, seq, place % 2, 1)
    over_x = lambda v: halve(v, "seq", 2, seq, place // 2, 0)
    over_y = lambda v: halve(v, "y", 1, 2, own_y, v.ndim - 3)
    sides = add_low(keep, over(send, "core")).reshape(2, nz, 2, share, -1)
    grad_query, grad_out = over_x(sides[..., :WIDTH]), over_y(sides[..., WIDTH:])
    (grad_w_down,) = outer_blocks(after(hidden, sides), [cots], "down_grads")
    grad_w_down = scatter_sum(grad_w_down, "seq")[:run].astype(F32)
    grad_w_gate = swap(after(grad_w_gate, terms), CTX).reshape(ctx, share, -1)
    (grad_pair,) = outer_blocks([normed], [[after(terms, grad_out, grad_query)]], "pair_grads")
    grad_tokens, norm_attn_sum, bias = tokens_back(
        core, jnp.concatenate([dq, after(terms, grad_pair)], axis=1), left, right, tokens, attn_gain, grad_middle
    )
    grad_pair, bias, forth, grad_w_gate = together(grad_pair, bias, forth, grad_w_gate)
    grad_w_up = swap(after(grad_w_up, grad_w_gate), CTX).reshape(ctx, share, -1)
    grad_pair = over_core(grad_pair.reshape(2, 2, nz, 2, share, -1))
    grad_out, grad_query = over_x(grad_out), over_y(grad_query)
    grad_w_up, grad_out, grad_query, grad_pair = together(grad_w_up, grad_out, grad_query, grad_pair)
    side = add_up(exchange_near(jnp.concatenate([grad_out, grad_query], axis=2), nz, own_z))
    grad_pair = add_up(exchange_near(over_y(over_x(grad_pair)), nz, own_z))
    grad_w_out, grad_w_query = side[:, :WIDTH], side[:, WIDTH:]
    grad_w_key, grad_w_value = grad_pair[:, :KV_WIDTH], grad_pair[:, KV_WIDTH:]
    output = middle + add_up(forth)
    grad_w_gate, grad_w_up = columns_in(grad_w_gate, grad_w_up, seq, ctx, run, padded)

    sums = sum_all(jnp.concatenate([norm_attn_sum, norm_mlp_sum, bias], axis=1), seq, nz)[0]
    number = place * ctx + index
    mine = lambda start, size: lax.dynamic_slice_in_dim(sums, start + number * size, size)
    g_norm_attn, g_norm_mlp, g_b_query = (mine(n * WIDTH, share) for n in range(3))
    g_b_key = sums[3 * WIDTH:3 * WIDTH + KV_WIDTH]
    g_b_value = mine(3 * WIDTH + KV_WIDTH, vshare)
    return (
        output,
        grad_tokens,
        grad_w_query,
        g_b_query,
        grad_w_key,
        g_b_key,
        grad_w_value,
        g_b_value,
        grad_w_out,
        g_norm_attn,
        grad_w_gate,
        grad_w_up,
        grad_w_down,
        g_norm_mlp,
    )


def solution(mesh):
    seq, ctx = mesh.shape["seq"], mesh.shape["ctx"]
    rows2, rows1 = P(ALL, None), P(ALL)
    return jax.shard_map(
        functools.partial(body, seq=seq, ctx=ctx),
        mesh=Mesh(mesh.devices.reshape(seq, ctx // 2, 2), ALL),
        in_specs=(
            rows2,
            P("seq", None),
            rows2,
            rows1,
            rows2,
            P(),
            rows2,
            rows1,
            rows2,
            rows1,
            rows2,
            rows2,
            rows2,
            rows1,
            rows2,
        ),
        out_specs=(
            rows2,
            rows2,
            rows2,
            rows1,
            rows2,
            P(),
            rows2,
            rows1,
            rows2,
            rows1,
            rows2,
            rows2,
            rows2,
            rows1,
        ),
        check_vma=False,
    )
```
